256 devices in a mesh: row: 8 (over x, z_hi), col: 8 (over y, core), tp: 4 (over z_lo).
Axes of the slice: x: 4, y: 4, z: 8 (z_hi: 2, z_lo: 4; z = z_hi * 4 + z_lo), core: 2. Of those that a mesh axis runs over, the one named last changes fastest.
Arguments:
- crop_rows: bfloat16 [8192, 1024], P(('row', 'col')), may hold values from -40 to 40
- up_weight: bfloat16 [1024, 4096], P(None, 'tp'), may hold values from -0.1875 to 0.1875
- down_weight: bfloat16 [4096, 1024], P('tp'), may hold values from -0.09375 to 0.09375
- proj_weight: bfloat16 [1024, 256], replicated, may hold values from -1 to 1
- prototypes: bfloat16 [262144, 256], P(('col', 'tp')), may hold values from -120 to 120
- partner: int32 [8192], P('row'), may hold values from 0 to 8191, as said below
Outputs:
- grad_prototypes: bfloat16 [262144, 256], P(('col', 'tp'))
The draws below stay inside these ranges and needn't reach their ends.
Inputs may be any that keep to these rules, and one draw needn't show every extreme that they name: partner is a permutation of the 8192 crops that keeps every crop inside its aligned block of 1024 crops.
All inputs are finite; a program needn't handle non-finite values.
Results may differ from the reference program's by a relative error of at most 0.018.
Values may be sent and summed in bfloat16 or wider, within the bound.
No kernel may reach another device: no remote copies, remote signals or barrier semaphores. Data moves between devices by JAX's collectives and lax.ppermute only.
A program may use at most 192 MiB of HBM per device.

```python
import math
import jax
import jax.numpy as jnp
from jax import lax

D = 1024
FF = 4096
E = 256
K_DEV = 8192
ITERS = 3
ROWS_HEAD = 1024
CROP_TOKENS = 8192
K = 262144
N_ROW = 8


def shared_directions(key):
    first, second = jax.random.split(key, 2)
    feature_dir = (jax.random.randint(first, (D,), 0, 2) * 2 - 1).astype(jnp.float32)
    embed_dir = (jax.random.randint(second, (E,), 0, 2) * 2 - 1).astype(jnp.float32)
    return (feature_dir, embed_dir)


def draw_crop_rows(key, part):
    feature_dir, embed_dir = shared_directions(key)
    key = jax.random.fold_in(key, 11)
    first, second, third, fourth = jax.random.split(key, 4)
    position = jnp.arange(CROP_TOKENS, dtype=jnp.float32)[:, None] / CROP_TOKENS
    jitter = jax.random.uniform(fourth, (CROP_TOKENS, 1), jnp.float32, 0.7, 1.3)
    base = jnp.clip(jax.random.normal(first, (CROP_TOKENS, D), jnp.float32), -4.0, 4.0)
    row_spread = jnp.exp(jax.random.uniform(second, (CROP_TOKENS, 1), jnp.float32, math.log(0.5), math.log(5.0)))
    column_spread = jnp.exp(jax.random.uniform(third, (1, D), jnp.float32, math.log(0.5), math.log(2.0)))
    strength = (0.2 + position) * jitter
    values = base * row_spread * column_spread + 3.0 * strength * feature_dir[None, :]
    return jnp.clip(values, -40.0, 40.0).astype(jnp.bfloat16)


def draw_proj_weight(key, part):
    feature_dir, embed_dir = shared_directions(key)
    key = jax.random.fold_in(key, 31)
    base = jnp.clip(jax.random.normal(key, (D, E), jnp.float32), -4.0, 4.0) * (1.0 / math.sqrt(D))
    values = base + 2.0 / D * feature_dir[:, None] * embed_dir[None, :]
    return values.astype(jnp.bfloat16)


def draw_prototypes(key, part):
    feature_dir, embed_dir = shared_directions(key)
    key = jax.random.fold_in(key, 23)
    first, second, third, fourth = jax.random.split(key, 4)
    position = jnp.arange(K, dtype=jnp.float32)[:, None] / K
    jitter = jax.random.uniform(fourth, (K, 1), jnp.float32, 0.7, 1.3)
    base = jnp.clip(jax.random.normal(first, (K, E), jnp.float32), -4.0, 4.0)
    row_spread = jnp.exp(jax.random.uniform(second, (K, 1), jnp.float32, 0.0, math.log(10.0)))
    column_spread = jnp.exp(jax.random.uniform(third, (1, E), jnp.float32, math.log(0.5), math.log(3.0)))
    strength = 1.5 * position * jitter
    values = row_spread * (base * column_spread + strength * embed_dir[None, :])
    return jnp.clip(values, -120.0, 120.0).astype(jnp.bfloat16)


def draw_partner(key, part):
    key = jax.random.fold_in(key, 29)
    groups = CROP_TOKENS // ROWS_HEAD
    group_keys = jax.random.split(key, groups)
    orders = jax.vmap(lambda group_key: jax.random.permutation(group_key, ROWS_HEAD))(group_keys)
    offsets = jnp.arange(groups, dtype=jnp.int32)[:, None] * ROWS_HEAD
    return (orders.astype(jnp.int32) + offsets).reshape(CROP_TOKENS)


def levels(own_key, dims, cuts, smallest, high):
    def one(axis_at, blocks):
        draws = jax.random.uniform(jax.random.fold_in(jax.random.fold_in(own_key, 6), axis_at), (blocks,), jnp.float32, smallest / len(cuts), high / len(cuts))
        return jnp.repeat(jnp.exp(draws), dims[axis_at] // blocks).reshape((-1,) + (1,) * (len(dims) - axis_at - 1))

    level = one(*cuts[0])
    for cut in cuts[1:]:
        level = level * one(*cut)
    return level


def noise(key, shape, deviation, limit, shards=(), kind=jnp.bfloat16):
    drawn = jax.random.normal(key, shape, jnp.float32) * deviation
    if len(shards) > 0:
        drawn = levels(key, shape, shards, -0.22, 0.18) * drawn
    return jnp.clip(drawn, min=-limit, max=limit).astype(kind)


def setup_inputs(seed: int = 0) -> dict:
    key_list = jax.random.split(jax.random.key(seed), 7)
    crop_rows = draw_crop_rows(jax.random.fold_in(key_list[6], 71), 0)
    up_weight = noise(key_list[1], (D, FF), D ** -0.5, 0.1875, ((1, 4),))
    down_weight = noise(key_list[2], (FF, D), FF ** -0.5, 0.09375, ((0, 4),))
    proj_weight = draw_proj_weight(jax.random.fold_in(key_list[6], 71), 0)
    prototypes = draw_prototypes(jax.random.fold_in(key_list[6], 71), 0)
    partner = draw_partner(jax.random.fold_in(key_list[6], 71), 0)
    return dict(crop_rows=crop_rows, up_weight=up_weight, down_weight=down_weight, proj_weight=proj_weight, prototypes=prototypes, partner=partner)


SOFTMAX_TEMPER = 0.1
SHARPNESS = 0.05

def unit_rows(matrix):
    square_mean = lax.optimization_barrier(jnp.mean(matrix * matrix, axis=-1, keepdims=True))
    return matrix * lax.rsqrt(matrix.shape[-1] * (square_mean + 1e-06))

def reference(crop_rows, up_weight, down_weight, proj_weight, prototypes, partner):
    crop_values = crop_rows.astype(jnp.float32)
    centred = crop_values - lax.optimization_barrier(jnp.mean(crop_values, axis=1, keepdims=True))
    normed = (centred * lax.rsqrt(lax.optimization_barrier(jnp.mean(centred * centred, axis=1, keepdims=True)) + 1e-05)).astype(jnp.bfloat16)
    hidden = jax.nn.gelu(jnp.dot(normed, up_weight, preferred_element_type=jnp.float32)).astype(jnp.bfloat16)
    branch_out = jnp.dot(hidden, down_weight, preferred_element_type=jnp.float32)
    raw_embed = jnp.dot(crop_values + branch_out, proj_weight.astype(jnp.float32), precision=lax.Precision.HIGHEST)
    embedding = unit_rows(raw_embed).astype(jnp.bfloat16)
    unit_protos = unit_rows(prototypes.astype(jnp.float32)).astype(jnp.bfloat16)
    prototype_block_list = unit_protos.reshape(K // K_DEV, K_DEV, E)
    raw_blocks = prototypes.astype(jnp.float32).reshape(K // K_DEV, K_DEV, E)

    def sink_block(prototype_matrix):
        score_matrix = jnp.dot(embedding, prototype_matrix.T, preferred_element_type=jnp.float32)
        return (jnp.exp(score_matrix / SHARPNESS).astype(jnp.bfloat16), score_matrix)

    def soft_block(score_matrix):
        return jnp.exp(score_matrix / SOFTMAX_TEMPER).astype(jnp.bfloat16)
    total_values = jnp.zeros((CROP_TOKENS,), jnp.float32)
    row_scale = jnp.ones((CROP_TOKENS,), jnp.float32)
    column_factor = jnp.zeros((K // K_DEV, K_DEV), jnp.float32)
    for iteration in range(ITERS):
        first = iteration == 0

        def balancing_update(running_value, prototype_matrix):
            row_acc, soft_acc = running_value
            sink_weight, score_matrix = sink_block(prototype_matrix)
            sink_values = sink_weight.astype(jnp.float32)
            column_part = 1.0 / lax.optimization_barrier(jnp.sum(sink_values * row_scale[:, None], axis=0))
            row_acc = row_acc + lax.optimization_barrier(jnp.sum(sink_values * column_part[None, :], axis=1))
            if first:
                soft_acc = soft_acc + lax.optimization_barrier(jnp.sum(soft_block(score_matrix).astype(jnp.float32), axis=1))
            return ((row_acc, soft_acc), column_part)
        (row_aggregate, softmax_aggregate), column_factor = lax.scan(balancing_update, (jnp.zeros((CROP_TOKENS,), jnp.float32), total_values), prototype_block_list)
        total_values = softmax_aggregate
        row_scale = 1.0 / row_aggregate
    out_scale = E / math.sqrt(CROP_TOKENS)

    def grad_block(inputs):
        prototype_matrix, columns, raw_rows = inputs
        sink_weight, score_matrix = sink_block(prototype_matrix)
        codes = row_scale[:, None] * sink_weight.astype(jnp.float32) * columns[None, :]
        target = jnp.take(codes, partner, axis=0)
        code_error = (K * (soft_block(score_matrix).astype(jnp.float32) / total_values[:, None] - target)).astype(jnp.bfloat16)
        grouped = jnp.einsum('gik,gie->gke', code_error.reshape(N_ROW, ROWS_HEAD, K_DEV).astype(jnp.float32), embedding.reshape(N_ROW, ROWS_HEAD, E).astype(jnp.float32))
        rounded = lax.optimization_barrier(grouped.astype(jnp.bfloat16)).astype(jnp.float32)
        summed = lax.optimization_barrier(jnp.sum(rounded, axis=0))
        square_mean = lax.optimization_barrier(jnp.mean(raw_rows * raw_rows, axis=1, keepdims=True))
        factor = lax.rsqrt(E * (square_mean + 1e-06))
        inner_prod = lax.optimization_barrier(jnp.sum(raw_rows * summed, axis=1, keepdims=True))
        gradient = factor * summed - factor * raw_rows * inner_prod / (E * (square_mean + 1e-06))
        return (out_scale * gradient).astype(jnp.bfloat16)
    pieces = lax.map(grad_block, (prototype_block_list, column_factor, raw_blocks))
    return pieces.reshape(K, E)
```

```python
import functools
import math

import jax
import jax.numpy as jnp
from jax import lax
from jax.experimental import pallas as pl
from jax.experimental.pallas import tpu as pltpu
from jax.sharding import PartitionSpec as P

ITERS = 3


SOFTMAX_TEMPER = 0.1
LOG2_E = 1.4426950408889634
CROP_STEP = 512
PROTO_STEP = 256


def unit_rows(matrix):
    square_mean = jnp.mean(matrix * matrix, axis=-1, keepdims=True)
    return matrix * lax.rsqrt(matrix.shape[-1] * (square_mean + 1e-06))


def broadcast_along(block, axes):
    count = lax.axis_size(axes)
    copies = jnp.broadcast_to(block, (count,) + block.shape)
    return lax.all_to_all(copies, axes, 0, 0, tiled=True)


def sum_along(block, axes):
    return jnp.sum(broadcast_along(block, axes), axis=0)


def pairwise_sum(block, axis):
    count = lax.axis_size(axis)
    terms = [block] + [
        lax.ppermute(block, axis, [(device, device ^ step) for device in range(count)])
        for step in range(1, count)
    ]
    while len(terms) > 1:
        terms = [terms[at] + terms[at + 1] for at in range(0, len(terms), 2)]
    return terms[0]


def total_sum(block):
    return sum_along(pairwise_sum(sum_along(block, "col"), "tp"), "row")


def weights_kernel(protos_ref, embed_ref, sink_ref, soft_ref, total_ref):
    embed = embed_ref[...]
    total = jnp.zeros((1, embed.shape[0]), jnp.float32)
    for start in range(0, protos_ref.shape[0], PROTO_STEP):
        rows = pl.ds(start, PROTO_STEP)
        score = lax.dot_general(
            protos_ref[rows, :], embed, (((1,), (1,)), ((), ())), preferred_element_type=jnp.float32
        )
        weight = jnp.exp2(score * (LOG2_E / SOFTMAX_TEMPER))
        soft_ref[rows, :] = weight.astype(jnp.bfloat16)
        sink_ref[rows, :] = (weight * weight).astype(jnp.bfloat16)
        total += jnp.sum(weight, axis=0, keepdims=True)
    total_ref[...] = total


def exp_weights(protos, embedding):
    count, width = protos.shape
    crops = embedding.shape[0]
    step = CROP_STEP
    return pl.pallas_call(
        weights_kernel,
        grid=(crops // step,),
        in_specs=[
            pl.BlockSpec((count, width), lambda at: (0, 0)),
            pl.BlockSpec((step, width), lambda at: (at, 0)),
        ],
        out_specs=[
            pl.BlockSpec((count, step), lambda at: (0, at)),
            pl.BlockSpec((count, step), lambda at: (0, at)),
            pl.BlockSpec((1, step), lambda at: (0, at)),
        ],
        out_shape=[
            jax.ShapeDtypeStruct((count, crops), jnp.bfloat16),
            jax.ShapeDtypeStruct((count, crops), jnp.bfloat16),
            jax.ShapeDtypeStruct((1, crops), jnp.float32),
        ],
        compiler_params=pltpu.CompilerParams(vmem_limit_bytes=40 << 20),
        name="exp_weights",
    )(protos, embedding)


def balance_kernel(scale_ref, sink_ref, row_ref, column_ref):
    crops = sink_ref.shape[1]
    rows = sink_ref.shape[0]
    lanes = 128
    part = jnp.zeros((rows, lanes), jnp.float32)
    for start in range(0, crops, lanes):
        columns = pl.ds(start, lanes)
        part += sink_ref[:, columns].astype(jnp.float32) * scale_ref[:, columns]
    column = 1.0 / jnp.sum(part, axis=1, keepdims=True)
    column_ref[...] = column
    across = jnp.broadcast_to(column, (rows, lanes)).T[:8, :]
    high = across.astype(jnp.bfloat16)
    low = (across - high.astype(jnp.float32)).astype(jnp.bfloat16)

    @pl.when(pl.program_id(0) == 0)
    def _():
        row_ref[...] = jnp.zeros_like(row_ref)

    both = jnp.concatenate([high[:8], low[:8]], axis=0)
    for start in range(0, crops, 2048):
        columns = pl.ds(start, 2048)
        product = jnp.dot(both, sink_ref[:, columns], preferred_element_type=jnp.float32)
        row_ref[:, columns] += product[0:1, :] + product[8:9, :]


def balance(row_scale, sink_weight):
    count, crops = sink_weight.shape
    return pl.pallas_call(
        balance_kernel,
        grid=(count // PROTO_STEP,),
        in_specs=[
            pl.BlockSpec((1, crops), lambda at: (0, 0)),
            pl.BlockSpec((PROTO_STEP, crops), lambda at: (at, 0)),
        ],
        out_specs=[
            pl.BlockSpec((1, crops), lambda at: (0, 0)),
            pl.BlockSpec((PROTO_STEP, 1), lambda at: (at, 0)),
        ],
        out_shape=[
            jax.ShapeDtypeStruct((1, crops), jnp.float32),
            jax.ShapeDtypeStruct((count, 1), jnp.float32),
        ],
        compiler_params=pltpu.CompilerParams(vmem_limit_bytes=40 << 20),
        name="balance",
    )(row_scale.reshape(1, crops), sink_weight)


def swap_kernel(partner_ref, embed_ref, out_ref):
    rows = embed_ref.shape[0]
    place = lax.broadcasted_iota(jnp.int32, (rows, rows), 0)
    chosen = jnp.where(place == partner_ref[0], 1.0, 0.0).astype(jnp.bfloat16)
    out_ref[...] = jnp.dot(chosen, embed_ref[...], preferred_element_type=jnp.float32).astype(
        jnp.bfloat16
    )


def swap_partners(local_partner, embedding):
    blocks, rows = local_partner.shape
    width = embedding.shape[1]
    return pl.pallas_call(
        swap_kernel,
        grid=(blocks,),
        in_specs=[
            pl.BlockSpec((1, 1, rows), lambda at: (at, 0, 0)),
            pl.BlockSpec((rows, width), lambda at: (at, 0)),
        ],
        out_specs=pl.BlockSpec((rows, width), lambda at: (at, 0)),
        out_shape=jax.ShapeDtypeStruct(embedding.shape, jnp.bfloat16),
        compiler_params=pltpu.CompilerParams(vmem_limit_bytes=40 << 20),
        name="swap_partners",
    )(local_partner.reshape(blocks, 1, rows), embedding)


def shards(crop_rows, up_weight, down_weight, proj_weight, prototypes, partner):
    tp_count = lax.axis_size("tp")
    col_count = lax.axis_size("col")
    row_count = lax.axis_size("row")
    crop_values = crop_rows.astype(jnp.float32)
    centred = crop_values - jnp.mean(crop_values, axis=1, keepdims=True)
    normed = (
        centred * lax.rsqrt(jnp.mean(centred * centred, axis=1, keepdims=True) + 1e-05)
    ).astype(jnp.bfloat16)
    hidden = jax.nn.gelu(jnp.dot(normed, up_weight, preferred_element_type=jnp.float32)).astype(
        jnp.bfloat16
    )
    branch_out = jnp.dot(hidden, down_weight, preferred_element_type=jnp.float32)
    partial_proj = jnp.dot(
        crop_values / tp_count + branch_out,
        proj_weight.astype(jnp.float32),
        precision=lax.Precision.HIGHEST,
    )
    embed_width = partial_proj.shape[1]
    local_raw = pairwise_sum(partial_proj, "tp")
    local_embed = unit_rows(local_raw).astype(jnp.bfloat16)
    row_embed = broadcast_along(local_embed, "col").reshape(-1, embed_width)
    embedding = broadcast_along(row_embed, "row").reshape(-1, embed_width)
    block_rows = partner.shape[0]
    partners = broadcast_along(partner, "row").reshape(row_count, block_rows)
    local_partner = partners - block_rows * jnp.arange(row_count, dtype=jnp.int32)[:, None]

    proto_total = prototypes.shape[0] * col_count * tp_count
    own_count = prototypes.shape[0] // row_count
    own_rows = lax.dynamic_slice_in_dim(
        prototypes, lax.axis_index("row") * own_count, own_count, 0
    )
    raw_rows = own_rows.astype(jnp.float32)
    unit_protos = unit_rows(raw_rows).astype(jnp.bfloat16)

    crops = embedding.shape[0]
    sink_weight, soft_weight, soft_part = exp_weights(unit_protos, embedding)
    row_scale = jnp.ones((crops,), jnp.float32)
    totals = None
    for iteration in range(ITERS):
        row_part, column_factor = balance(row_scale, sink_weight)
        if iteration == 0:
            sums = total_sum(jnp.concatenate([row_part, soft_part], axis=0))
            row_sum, totals = sums[0], sums[1]
        else:
            row_sum = total_sum(row_part)[0]
        row_scale = 1.0 / row_sum

    swapped = swap_partners(local_partner, embedding)
    soft_rows = (embedding.astype(jnp.float32) / totals[:, None]).astype(jnp.bfloat16)
    target_rows = (swapped.astype(jnp.float32) * row_scale[:, None]).astype(jnp.bfloat16)
    soft_sum = jnp.dot(soft_weight, soft_rows, preferred_element_type=jnp.float32)
    target_sum = jnp.dot(sink_weight, target_rows, preferred_element_type=jnp.float32)
    summed = proto_total * (soft_sum - column_factor * target_sum)

    square_mean = jnp.mean(raw_rows * raw_rows, axis=1, keepdims=True)
    factor = lax.rsqrt(embed_width * (square_mean + 1e-06))
    inner_prod = jnp.sum(raw_rows * summed, axis=1, keepdims=True)
    gradient = factor * summed - factor * raw_rows * inner_prod / (
        embed_width * (square_mean + 1e-06)
    )
    out_scale = embed_width / math.sqrt(crops)
    own_gradient = (out_scale * gradient).astype(jnp.bfloat16)
    return broadcast_along(own_gradient, "row").reshape(-1, embed_width)


def solution(mesh):
    return jax.shard_map(
        shards,
        mesh=mesh,
        in_specs=(
            P(("row", "col"), None),
            P(None, "tp"),
            P("tp", None),
            P(),
            P(("col", "tp"), None),
            P("row"),
        ),
        out_specs=P(("col", "tp"), None),
        check_vma=False,
    )
```

```python
import functools
import math

import jax
import jax.numpy as jnp
from jax import lax
from jax.experimental import pallas as pl
from jax.experimental.pallas import tpu as pltpu
from jax.sharding import PartitionSpec as P

ITERS = 3


SOFTMAX_TEMPER = 0.1
LOG2_E = 1.4426950408889634
CROP_STEP = 512
PROTO_STEP = 256


def unit_rows(matrix):
    square_mean = jnp.mean(matrix * matrix, axis=-1, keepdims=True)
    return matrix * lax.rsqrt(matrix.shape[-1] * (square_mean + 1e-06))


def shifted(block, axis, target):
    count = lax.axis_size(axis)
    return lax.ppermute(block, axis, [(device, target(device) % count) for device in range(count)])


def placed(pieces, count):
    rows = pieces[0][0].shape
    result = jnp.zeros((count,) + rows, pieces[0][0].dtype)
    for piece, place in pieces:
        result = lax.dynamic_update_slice_in_dim(result, piece[None], place, 0)
    return result


def pairwise_sum(block, axis):
    count = lax.axis_size(axis)
    terms = [block] + [
        shifted(block, axis, lambda device, step=step: device ^ step) for step in range(1, count)
    ]
    while len(terms) > 1:
        terms = [terms[at] + terms[at + 1] for at in range(0, len(terms), 2)]
    return terms[0]


def broadcast_along(block, axes):
    count = lax.axis_size(axes)
    copies = jnp.broadcast_to(block, (count,) + block.shape)
    return lax.all_to_all(copies, axes, 0, 0, tiled=True)


def total_sum(parts):
    count, crops = parts.shape
    cols = lax.axis_size("col")
    share = crops // cols
    scattered = jnp.swapaxes(parts.reshape(count, cols, share), 0, 1).reshape(cols, count * share)
    own = jnp.sum(lax.all_to_all(scattered, "col", 0, 0, tiled=True), axis=0)
    own = jnp.sum(broadcast_along(own, ("row", "tp")), axis=0)
    gathered = broadcast_along(own, "col").reshape(cols, count, share)
    return jnp.swapaxes(gathered, 0, 1).reshape(count, crops)


def gather_embeddings(local_embed):
    row, col = lax.axis_index("row"), lax.axis_index("col")
    far = shifted(local_embed, "row", lambda device: device ^ 1)
    pair = placed([(local_embed, row % 2), (far, 1 - row % 2)], 2)
    line = [
        (pair, row // 2),
        (shifted(pair, "row", lambda device: device + 2), (row // 2 + 3) % 4),
        (shifted(pair, "row", lambda device: device - 2), (row // 2 + 1) % 4),
        (shifted(pair, "row", lambda device: device + 4), (row // 2 + 2) % 4),
    ]
    block = placed(line, 4).reshape(-1, local_embed.shape[1])
    ups = [
        (col, block),
        ((col + 6) % 8, shifted(block, "col", lambda device: device + 2)),
        ((col + 2) % 8, shifted(block, "col", lambda device: device - 2)),
        ((col + 4) % 8, shifted(block, "col", lambda device: device + 4)),
    ]
    arrived = []
    for place, piece in ups:
        arrived.append((place, piece))
        arrived.append((place ^ 1, shifted(piece, "col", lambda device: device ^ 1)))
    return arrived


def gather_rows(own):
    row = lax.axis_index("row")
    half = own.shape[0] // 2
    far = [
        shifted(own[:half], "row", lambda device: device ^ 1),
        shifted(own[half:], "row", lambda device: device ^ 1),
    ]
    result = jnp.zeros((8,) + own.shape, own.dtype)

    def put(result, piece, place, start):
        return lax.dynamic_update_slice(result, piece[None], (place % 8, start, 0))

    result = put(result, own, row, 0)
    for piece, place, start in ((own, row, 0), (far[0], row ^ 1, 0), (far[1], row ^ 1, half)):
        middle = piece.shape[0] // 2
        right = shifted(piece, "row", lambda device: device + 2)
        left = shifted(piece, "row", lambda device: device - 2)
        right_on = shifted(right[:middle], "row", lambda device: device + 2)
        left_on = shifted(left[middle:], "row", lambda device: device - 2)
        result = put(result, piece, place, start)
        result = put(result, right, place + 6, start)
        result = put(result, left, place + 2, start)
        result = put(result, right_on, place + 4, start)
        result = put(result, left_on, place + 4, start + middle)
    return result.reshape(-1, own.shape[1])


def weights_kernel(place_ref, protos_ref, embed_ref, *refs):
    sink_ref, soft_ref, total_ref, copy_ref = refs[-4:]
    embed = embed_ref[...]
    copy_ref[...] = embed
    total = jnp.zeros((1, embed.shape[0]), jnp.float32)
    for start in range(0, protos_ref.shape[0], PROTO_STEP):
        rows = pl.ds(start, PROTO_STEP)
        score = lax.dot_general(
            protos_ref[rows, :], embed, (((1,), (1,)), ((), ())), preferred_element_type=jnp.float32
        )
        weight = jnp.exp2(score * (LOG2_E / SOFTMAX_TEMPER))
        soft_ref[rows, :] = weight.astype(jnp.bfloat16)
        sink_ref[rows, :] = (weight * weight).astype(jnp.bfloat16)
        total += jnp.sum(weight, axis=0, keepdims=True)
    total_ref[...] = total


def exp_weights(place, protos, block, crops, before):
    count, width = protos.shape
    step = CROP_STEP
    steps = block.shape[0] // step
    shapes = [
        jax.ShapeDtypeStruct((count, crops), jnp.bfloat16),
        jax.ShapeDtypeStruct((count, crops), jnp.bfloat16),
        jax.ShapeDtypeStruct((1, crops), jnp.float32),
        jax.ShapeDtypeStruct((crops, width), jnp.bfloat16),
    ]
    return pl.pallas_call(
        weights_kernel,
        grid_spec=pltpu.PrefetchScalarGridSpec(
            num_scalar_prefetch=1,
            grid=(steps,),
            in_specs=[
                pl.BlockSpec((count, width), lambda at, place: (0, 0)),
                pl.BlockSpec((step, width), lambda at, place: (at, 0)),
            ]
            + [pl.BlockSpec(memory_space=pl.ANY)] * len(before),
            out_specs=[
                pl.BlockSpec((count, step), lambda at, place: (0, place[0] * steps + at)),
                pl.BlockSpec((count, step), lambda at, place: (0, place[0] * steps + at)),
                pl.BlockSpec((1, step), lambda at, place: (0, place[0] * steps + at)),
                pl.BlockSpec((step, width), lambda at, place: (place[0] * steps + at, 0)),
            ],
        ),
        out_shape=shapes,
        input_output_aliases={3 + at: at for at in range(len(before))},
        compiler_params=pltpu.CompilerParams(vmem_limit_bytes=40 << 20),
        name="exp_weights",
    )(place.reshape(1).astype(jnp.int32), protos, block, *before)


def balance_kernel(scale_ref, sink_ref, row_ref, column_ref):
    crops = sink_ref.shape[1]
    rows = sink_ref.shape[0]
    lanes = 128
    part = jnp.zeros((rows, lanes), jnp.float32)
    for start in range(0, crops, lanes):
        columns = pl.ds(start, lanes)
        part += sink_ref[:, columns].astype(jnp.float32) * scale_ref[:, columns]
    column = 1.0 / jnp.sum(part, axis=1, keepdims=True)
    column_ref[...] = column
    across = jnp.broadcast_to(column, (rows, lanes)).T[:8, :]
    high = across.astype(jnp.bfloat16)
    low = (across - high.astype(jnp.float32)).astype(jnp.bfloat16)

    @pl.when(pl.program_id(0) == 0)
    def _():
        row_ref[...] = jnp.zeros_like(row_ref)

    both = jnp.concatenate([high[:8], low[:8]], axis=0)
    for start in range(0, crops, 2048):
        columns = pl.ds(start, 2048)
        product = jnp.dot(both, sink_ref[:, columns], preferred_element_type=jnp.float32)
        row_ref[:, columns] += product[0:1, :] + product[8:9, :]


def balance(row_scale, sink_weight):
    count, crops = sink_weight.shape
    return pl.pallas_call(
        balance_kernel,
        grid=(count // PROTO_STEP,),
        in_specs=[
            pl.BlockSpec((1, crops), lambda at: (0, 0)),
            pl.BlockSpec((PROTO_STEP, crops), lambda at: (at, 0)),
        ],
        out_specs=[
            pl.BlockSpec((1, crops), lambda at: (0, 0)),
            pl.BlockSpec((PROTO_STEP, 1), lambda at: (at, 0)),
        ],
        out_shape=[
            jax.ShapeDtypeStruct((1, crops), jnp.float32),
            jax.ShapeDtypeStruct((count, 1), jnp.float32),
        ],
        compiler_params=pltpu.CompilerParams(vmem_limit_bytes=40 << 20),
        name="balance",
    )(row_scale.reshape(1, crops), sink_weight)


def swap_kernel(partner_ref, embed_ref, out_ref):
    cols, _, share, width = embed_ref.shape
    rows = cols * share
    place = lax.broadcasted_iota(jnp.int32, (rows, rows), 0)
    chosen = jnp.where(place == partner_ref[0], 1.0, 0.0).astype(jnp.bfloat16)
    embed = embed_ref[...].reshape(rows, width)
    swapped = jnp.dot(chosen, embed, preferred_element_type=jnp.float32)
    out_ref[...] = swapped.astype(jnp.bfloat16).reshape(embed_ref.shape)


def swap_partners(local_partner, embedding):
    blocks, rows = local_partner.shape
    width = embedding.shape[1]
    cols = lax.axis_size("col")
    split = (cols, blocks, rows // cols, width)
    spec = pl.BlockSpec((cols, 1, rows // cols, width), lambda at: (0, at, 0, 0))
    return pl.pallas_call(
        swap_kernel,
        grid=(blocks,),
        in_specs=[pl.BlockSpec((1, 1, rows), lambda at: (at, 0, 0)), spec],
        out_specs=spec,
        out_shape=jax.ShapeDtypeStruct(split, jnp.bfloat16),
        compiler_params=pltpu.CompilerParams(vmem_limit_bytes=40 << 20),
        name="swap_partners",
    )(local_partner.reshape(blocks, 1, rows), embedding.reshape(split)).reshape(embedding.shape)


def shards(crop_rows, up_weight, down_weight, proj_weight, prototypes, partner):
    tp_count = lax.axis_size("tp")
    col_count = lax.axis_size("col")
    row_count = lax.axis_size("row")
    crop_values = crop_rows.astype(jnp.float32)
    centred = crop_values - jnp.mean(crop_values, axis=1, keepdims=True)
    normed = (
        centred * lax.rsqrt(jnp.mean(centred * centred, axis=1, keepdims=True) + 1e-05)
    ).astype(jnp.bfloat16)
    hidden = jax.nn.gelu(jnp.dot(normed, up_weight, preferred_element_type=jnp.float32)).astype(
        jnp.bfloat16
    )
    branch_out = jnp.dot(hidden, down_weight, preferred_element_type=jnp.float32)
    partial_proj = jnp.dot(
        crop_values / tp_count + branch_out,
        proj_weight.astype(jnp.float32),
        precision=lax.Precision.HIGHEST,
    )
    embed_width = partial_proj.shape[1]
    local_raw = pairwise_sum(partial_proj, "tp")
    local_embed = unit_rows(local_raw).astype(jnp.bfloat16)
    block_rows = partner.shape[0]
    partners = broadcast_along(partner, "row").reshape(row_count, block_rows)
    local_partner = partners - block_rows * jnp.arange(row_count, dtype=jnp.int32)[:, None]

    proto_total = prototypes.shape[0] * col_count * tp_count
    own_count = prototypes.shape[0] // row_count
    own_rows = lax.dynamic_slice_in_dim(
        prototypes, lax.axis_index("row") * own_count, own_count, 0
    )
    raw_rows = own_rows.astype(jnp.float32)
    unit_protos = unit_rows(raw_rows).astype(jnp.bfloat16)

    crops = row_count * block_rows
    weights = []
    for place, block in gather_embeddings(local_embed):
        weights = exp_weights(place, unit_protos, block, crops, weights)
    sink_weight, soft_weight, soft_part, embedding = weights
    row_scale = jnp.ones((crops,), jnp.float32)
    totals = None
    for iteration in range(ITERS):
        row_part, column_factor = balance(row_scale, sink_weight)
        if iteration == 0:
            sums = total_sum(jnp.concatenate([row_part, soft_part], axis=0))
            row_sum, totals = sums[0], sums[1]
        else:
            row_sum = total_sum(row_part)[0]
        row_scale = 1.0 / row_sum

    swapped = swap_partners(local_partner, embedding)
    soft_rows = (embedding.astype(jnp.float32) / totals[:, None]).astype(jnp.bfloat16)
    target_rows = (swapped.astype(jnp.float32) * row_scale[:, None]).astype(jnp.bfloat16)
    soft_sum = jnp.dot(soft_weight, soft_rows, preferred_element_type=jnp.float32)
    target_sum = jnp.dot(sink_weight, target_rows, preferred_element_type=jnp.float32)
    summed = proto_total * (soft_sum - column_factor * target_sum)

    square_mean = jnp.mean(raw_rows * raw_rows, axis=1, keepdims=True)
    factor = lax.rsqrt(embed_width * (square_mean + 1e-06))
    inner_prod = jnp.sum(raw_rows * summed, axis=1, keepdims=True)
    gradient = factor * summed - factor * raw_rows * inner_prod / (
        embed_width * (square_mean + 1e-06)
    )
    out_scale = embed_width / math.sqrt(crops)
    own_gradient = (out_scale * gradient).astype(jnp.bfloat16)
    return gather_rows(own_gradient)


def solution(mesh):
    return jax.shard_map(
        shards,
        mesh=mesh,
        in_specs=(
            P(("row", "col"), None),
            P(None, "tp"),
            P("tp", None),
            P(),
            P(("col", "tp"), None),
            P("row"),
        ),
        out_specs=P(("col", "tp"), None),
        check_vma=False,
    )
```

```python
import functools
import math

import jax
import jax.numpy as jnp
from jax import lax
from jax.experimental import pallas as pl
from jax.experimental.pallas import tpu as pltpu
from jax.sharding import PartitionSpec as P

ITERS = 3


SOFTMAX_TEMPER = 0.1
LOG2_E = 1.4426950408889634
CROP_STEP = 512
PROTO_STEP = 256


def unit_rows(matrix):
    square_mean = jnp.mean(matrix * matrix, axis=-1, keepdims=True)
    return matrix * lax.rsqrt(matrix.shape[-1] * (square_mean + 1e-06))


def shifted(block, axis, target):
    count = lax.axis_size(axis)
    return lax.ppermute(block, axis, [(device, target(device) % count) for device in range(count)])


def placed(pieces, count):
    rows = pieces[0][0].shape
    result = jnp.zeros((count,) + rows, pieces[0][0].dtype)
    for piece, place in pieces:
        result = lax.dynamic_update_slice_in_dim(result, piece[None], place, 0)
    return result


def pairwise_sum(block, axis):
    count = lax.axis_size(axis)
    terms = [block] + [
        shifted(block, axis, lambda device, step=step: device ^ step) for step in range(1, count)
    ]
    while len(terms) > 1:
        terms = [terms[at] + terms[at + 1] for at in range(0, len(terms), 2)]
    return terms[0]


def broadcast_along(block, axes):
    count = lax.axis_size(axes)
    copies = jnp.broadcast_to(block, (count,) + block.shape)
    return lax.all_to_all(copies, axes, 0, 0, tiled=True)


def together(*values):
    return lax.optimization_barrier(values)


def total_sum(parts, beside=None, inputs=()):
    count, crops = parts.shape
    cols = lax.axis_size("col")
    share = crops // cols
    scattered = jnp.swapaxes(parts.reshape(count, cols, share), 0, 1).reshape(cols, count * share)
    own = jnp.sum(lax.all_to_all(scattered, "col", 0, 0, tiled=True), axis=0)
    own = own.astype(jnp.bfloat16)
    result = None
    if beside is not None:
        own, *inputs = together(own, *inputs)
    terms = broadcast_along(own, ("row", "tp"))
    if beside is not None:
        terms, result = together(terms, beside(*inputs))
    own = jnp.sum(terms.astype(jnp.float32), axis=0)
    gathered = broadcast_along(own, "col").reshape(cols, count, share)
    return jnp.swapaxes(gathered, 0, 1).reshape(count, crops), result


def gather_embeddings(local_embed, weigh):
    row, col = lax.axis_index("row"), lax.axis_index("col")
    far = shifted(local_embed, "row", lambda device: device ^ 1)
    pair = placed([(local_embed, row % 2), (far, 1 - row % 2)], 2)
    line = [
        (pair, row // 2),
        (shifted(pair, "row", lambda device: device + 2), (row // 2 + 3) % 4),
        (shifted(pair, "row", lambda device: device - 2), (row // 2 + 1) % 4),
        (shifted(pair, "row", lambda device: device + 4), (row // 2 + 2) % 4),
    ]
    block = placed(line, 4).reshape(-1, local_embed.shape[1])
    swap = lambda piece: shifted(piece, "col", lambda device: device ^ 1)
    others = [
        ((col + 6) % 8, shifted(block, "col", lambda device: device + 2)),
        ((col + 2) % 8, shifted(block, "col", lambda device: device - 2)),
        ((col + 4) % 8, shifted(block, "col", lambda device: device + 4)),
    ]
    twin = swap(block)
    weights = weigh(col, block, [])
    weights = weigh(col ^ 1, twin, weights)
    for place, piece in others:
        piece, weights[2] = together(piece, weights[2])
        twin = swap(piece)
        weights = weigh(place, piece, weights)
        weights = weigh(place ^ 1, twin, weights)
    return weights


def first_kernel(place_ref, own_ref, out_ref):
    out_ref[0] = own_ref[...]


def first_placed(own, place, count):
    rows, width = own.shape
    return pl.pallas_call(
        first_kernel,
        grid_spec=pltpu.PrefetchScalarGridSpec(
            num_scalar_prefetch=1,
            grid=(1,),
            in_specs=[pl.BlockSpec((rows, width), lambda at, place: (0, 0))],
            out_specs=pl.BlockSpec((1, rows, width), lambda at, place: (place[0], 0, 0)),
        ),
        out_shape=jax.ShapeDtypeStruct((count, rows, width), own.dtype),
        name="first_placed",
    )(place.reshape(1).astype(jnp.int32), own)


def gather_rows(own):
    row = lax.axis_index("row")
    half = own.shape[0] // 2
    quarter = half // 2
    over = row ^ 1
    flip = lambda block: shifted(block, "row", lambda device: device ^ 1)
    right = lambda block: shifted(block, "row", lambda device: device + 2)
    left = lambda block: shifted(block, "row", lambda device: device - 2)
    far0, far1, near_r, near_l = flip(own[:half]), flip(own[half:]), right(own), left(own)

    def put(result, piece, place, start):
        return lax.dynamic_update_slice(result, piece[None], (place & 7, start, 0))

    result = first_placed(own, row, 8)
    far0, near_r, near_l = together(far0, near_r, near_l)
    opp_r, opp_l = right(near_r[:half]), left(near_l[half:])
    far0_r, far0_l = right(far0), left(far0)
    result = put(result, near_r, row + 6, 0)
    result = put(result, near_l, row + 2, 0)
    result = put(result, far0, over, 0)
    result, far1, opp_r, opp_l, far0_r, far0_l = together(
        result, far1, opp_r, opp_l, far0_r, far0_l
    )
    far1_r, far1_l = right(far1), left(far1)
    far0_or, far0_ol = right(far0_r[:quarter]), left(far0_l[quarter:])
    result = put(result, opp_r, row + 4, 0)
    result = put(result, opp_l, row + 4, half)
    result = put(result, far0_r, over + 6, 0)
    result = put(result, far0_l, over + 2, 0)
    result = put(result, far1, over, half)
    result, far1_r, far1_l, far0_or, far0_ol = together(result, far1_r, far1_l, far0_or, far0_ol)
    far1_or, far1_ol = right(far1_r[:quarter]), left(far1_l[quarter:])
    result = put(result, far0_or, over + 4, 0)
    result = put(result, far0_ol, over + 4, quarter)
    result = put(result, far1_r, over + 6, half)
    result = put(result, far1_l, over + 2, half)
    result, far1_or, far1_ol = together(result, far1_or, far1_ol)
    result = put(result, far1_or, over + 4, half)
    result = put(result, far1_ol, over + 4, half + quarter)
    return result.reshape(-1, own.shape[1])


def weights_kernel(place_ref, protos_ref, embed_ref, *refs):
    sink_ref, soft_ref, total_ref, copy_ref = refs[-4:]
    embed = embed_ref[...]
    copy_ref[...] = embed
    total = jnp.zeros((1, embed.shape[0]), jnp.float32)
    for start in range(0, protos_ref.shape[0], PROTO_STEP):
        rows = pl.ds(start, PROTO_STEP)
        score = lax.dot_general(
            protos_ref[rows, :], embed, (((1,), (1,)), ((), ())), preferred_element_type=jnp.float32
        )
        weight = jnp.exp2(score * (LOG2_E / SOFTMAX_TEMPER))
        soft_ref[rows, :] = weight.astype(jnp.bfloat16)
        sink_ref[rows, :] = (weight * weight).astype(jnp.bfloat16)
        total += jnp.sum(weight, axis=0, keepdims=True)
    total_ref[...] = total


def exp_weights(place, protos, block, crops, before):
    count, width = protos.shape
    step = CROP_STEP
    steps = block.shape[0] // step
    shapes = [
        jax.ShapeDtypeStruct((count, crops), jnp.bfloat16),
        jax.ShapeDtypeStruct((count, crops), jnp.bfloat16),
        jax.ShapeDtypeStruct((1, crops), jnp.float32),
        jax.ShapeDtypeStruct((crops, width), jnp.bfloat16),
    ]
    return pl.pallas_call(
        weights_kernel,
        grid_spec=pltpu.PrefetchScalarGridSpec(
            num_scalar_prefetch=1,
            grid=(steps,),
            in_specs=[
                pl.BlockSpec((count, width), lambda at, place: (0, 0)),
                pl.BlockSpec((step, width), lambda at, place: (at, 0)),
            ]
            + [pl.BlockSpec(memory_space=pl.ANY)] * len(before),
            out_specs=[
                pl.BlockSpec((count, step), lambda at, place: (0, place[0] * steps + at)),
                pl.BlockSpec((count, step), lambda at, place: (0, place[0] * steps + at)),
                pl.BlockSpec((1, step), lambda at, place: (0, place[0] * steps + at)),
                pl.BlockSpec((step, width), lambda at, place: (place[0] * steps + at, 0)),
            ],
        ),
        out_shape=shapes,
        input_output_aliases={3 + at: at for at in range(len(before))},
        compiler_params=pltpu.CompilerParams(vmem_limit_bytes=60 << 20),
        cost_estimate=pl.CostEstimate(
            flops=2 * count * block.shape[0] * width,
            bytes_accessed=8 * count * block.shape[0],
            transcendentals=count * block.shape[0],
        ),
        name="exp_weights",
    )(place.reshape(1).astype(jnp.int32), protos, block, *before)


def balance_kernel(scale_ref, sink_hbm, row_ref, column_ref, held, sums, landed):
    count, crops = held.shape
    rows, lanes, stride = 128, 128, 1024
    blocks = count // rows
    copies = []
    for at in range(blocks):
        span = pl.ds(at * rows, rows)
        copies.append(pltpu.make_async_copy(sink_hbm.at[span], held.at[span], landed.at[at]))
        copies[at].start()
    both = None
    for at in range(blocks + 1):
        if at < blocks:
            copies[at].wait()

        def step(index, part, at=at, both=both):
            start = pl.multiple_of(index * stride, stride)
            columns = pl.ds(start, stride)
            if at > 0:
                product = jnp.dot(
                    both,
                    held[pl.ds((at - 1) * rows, rows), columns],
                    preferred_element_type=jnp.float32,
                )
                if at == 1:
                    sums[:, columns] = product
                else:
                    sums[:, columns] += product
            if at < blocks:
                for inner in range(0, stride, lanes):
                    tile = pl.ds(pl.multiple_of(start + inner, lanes), lanes)
                    values = held[pl.ds(at * rows, rows), tile].astype(jnp.float32)
                    part = part + values * scale_ref[:, tile]
            return part

        part = lax.fori_loop(0, crops // stride, step, jnp.zeros((rows, lanes), jnp.float32))
        if at < blocks:
            column = 1.0 / jnp.sum(part, axis=1, keepdims=True)
            column_ref[pl.ds(at * rows, rows), :] = column
            across = jnp.broadcast_to(column, (rows, lanes)).T[:8, :]
            high = across.astype(jnp.bfloat16)
            low = (across - high.astype(jnp.float32)).astype(jnp.bfloat16)
            both = jnp.concatenate([high, low], axis=0)
    row_ref[...] = sums[0:1, :] + sums[8:9, :]


def balance(row_scale, sink_weight):
    count, crops = sink_weight.shape
    return pl.pallas_call(
        balance_kernel,
        in_specs=[
            pl.BlockSpec(memory_space=pltpu.VMEM),
            pl.BlockSpec(memory_space=pl.ANY),
        ],
        out_specs=[pl.BlockSpec(memory_space=pltpu.VMEM)] * 2,
        out_shape=[
            jax.ShapeDtypeStruct((1, crops), jnp.float32),
            jax.ShapeDtypeStruct((count, 1), jnp.float32),
        ],
        scratch_shapes=[
            pltpu.VMEM((count, crops), jnp.bfloat16),
            pltpu.VMEM((16, crops), jnp.float32),
            pltpu.SemaphoreType.DMA((count // 128,)),
        ],
        compiler_params=pltpu.CompilerParams(vmem_limit_bytes=40 << 20),
        cost_estimate=pl.CostEstimate(
            flops=4 * count * crops, bytes_accessed=2 * count * crops, transcendentals=0
        ),
        name="balance",
    )(row_scale.reshape(1, crops), sink_weight)


def product_kernel(scale_ref, rows_ref, weight_ref, out_ref, scaled):
    lanes = 128

    @pl.when(pl.program_id(0) == 0)
    def _():
        def step(index, unused):
            span = pl.ds(pl.multiple_of(index * lanes, lanes), lanes)
            scale = jnp.broadcast_to(scale_ref[:, span], (lanes, lanes)).T
            for start in range(0, rows_ref.shape[1], lanes):
                columns = pl.ds(start, lanes)
                scaled[span, columns] = (
                    rows_ref[span, columns].astype(jnp.float32) * scale
                ).astype(jnp.bfloat16)
            return unused

        lax.fori_loop(0, rows_ref.shape[0] // lanes, step, 0)

    out_ref[...] = jnp.dot(weight_ref[...], scaled[...], preferred_element_type=jnp.float32)


def scaled_product(weight, scale, rows):
    count, crops = weight.shape
    width = rows.shape[1]
    return pl.pallas_call(
        product_kernel,
        grid=(count // PROTO_STEP,),
        in_specs=[
            pl.BlockSpec((1, crops), lambda at: (0, 0)),
            pl.BlockSpec((crops, width), lambda at: (0, 0)),
            pl.BlockSpec((PROTO_STEP, crops), lambda at: (at, 0)),
        ],
        out_specs=pl.BlockSpec((PROTO_STEP, width), lambda at: (at, 0)),
        out_shape=jax.ShapeDtypeStruct((count, width), jnp.float32),
        scratch_shapes=[pltpu.VMEM((crops, width), jnp.bfloat16)],
        compiler_params=pltpu.CompilerParams(vmem_limit_bytes=40 << 20),
        cost_estimate=pl.CostEstimate(
            flops=2 * count * crops * width,
            bytes_accessed=2 * count * crops + 2 * crops * width,
            transcendentals=0,
        ),
        name="scaled_product",
    )(scale.reshape(1, crops), rows, weight)


def swap_kernel(partner_ref, embed_ref, out_ref):
    cols, _, share, width = embed_ref.shape
    rows = cols * share
    place = lax.broadcasted_iota(jnp.int32, (rows, rows), 0)
    chosen = jnp.where(place == partner_ref[0], 1.0, 0.0).astype(jnp.bfloat16)
    embed = embed_ref[...].reshape(rows, width)
    swapped = jnp.dot(chosen, embed, preferred_element_type=jnp.float32)
    out_ref[...] = swapped.astype(jnp.bfloat16).reshape(embed_ref.shape)


def swap_partners(local_partner, embedding):
    blocks, rows = local_partner.shape
    width = embedding.shape[1]
    cols = lax.axis_size("col")
    split = (cols, blocks, rows // cols, width)
    spec = pl.BlockSpec((cols, 1, rows // cols, width), lambda at: (0, at, 0, 0))
    return pl.pallas_call(
        swap_kernel,
        grid=(blocks,),
        in_specs=[pl.BlockSpec((1, 1, rows), lambda at: (at, 0, 0)), spec],
        out_specs=spec,
        out_shape=jax.ShapeDtypeStruct(split, jnp.bfloat16),
        compiler_params=pltpu.CompilerParams(vmem_limit_bytes=40 << 20),
        cost_estimate=pl.CostEstimate(
            flops=2 * blocks * rows * rows * width,
            bytes_accessed=16 * blocks * rows * width,
            transcendentals=0,
        ),
        name="swap_partners",
    )(local_partner.reshape(blocks, 1, rows), embedding.reshape(split)).reshape(embedding.shape)


def shards(crop_rows, up_weight, down_weight, proj_weight, prototypes, partner):
    tp_count = lax.axis_size("tp")
    col_count = lax.axis_size("col")
    row_count = lax.axis_size("row")
    crop_values = crop_rows.astype(jnp.float32)
    centred = crop_values - jnp.mean(crop_values, axis=1, keepdims=True)
    normed = (
        centred * lax.rsqrt(jnp.mean(centred * centred, axis=1, keepdims=True) + 1e-05)
    ).astype(jnp.bfloat16)
    hidden = jax.nn.gelu(jnp.dot(normed, up_weight, preferred_element_type=jnp.float32)).astype(
        jnp.bfloat16
    )
    branch_out = jnp.dot(hidden, down_weight, preferred_element_type=jnp.float32)
    partial_proj = jnp.dot(
        crop_values / tp_count + branch_out,
        proj_weight.astype(jnp.float32),
        precision=lax.Precision.HIGHEST,
    )
    embed_width = partial_proj.shape[1]
    block_rows = partner.shape[0]
    partners = broadcast_along(partner, "row").reshape(row_count, block_rows)
    partial_proj, partners = together(partial_proj, partners)
    local_partner = partners - block_rows * jnp.arange(row_count, dtype=jnp.int32)[:, None]
    proto_total = prototypes.shape[0] * col_count * tp_count
    own_count = prototypes.shape[0] // row_count
    own_rows = lax.dynamic_slice_in_dim(
        prototypes, lax.axis_index("row") * own_count, own_count, 0
    )
    raw_rows = own_rows.astype(jnp.float32)
    unit_protos = unit_rows(raw_rows).astype(jnp.bfloat16)

    local_raw, unit_protos = together(pairwise_sum(partial_proj, "tp"), unit_protos)
    local_embed = unit_rows(local_raw).astype(jnp.bfloat16)

    crops = row_count * block_rows
    weights = gather_embeddings(
        local_embed,
        lambda place, block, before: list(exp_weights(place, unit_protos, block, crops, before)),
    )
    sink_weight, soft_weight, soft_part, embedding = weights
    row_scale = jnp.ones((crops,), jnp.float32)
    for iteration in range(ITERS):
        row_part, column_factor = balance(row_scale, sink_weight)
        if iteration == 0:
            sums, _ = total_sum(jnp.concatenate([row_part, soft_part], axis=0))
            row_sum, soft_scale = sums[0], 1.0 / sums[1]
        elif iteration == 1:
            sums, soft_sum = total_sum(
                row_part, scaled_product, (soft_weight, soft_scale, embedding)
            )
            row_sum = sums[0]
        else:
            sums, swapped = total_sum(row_part, swap_partners, (local_partner, embedding))
            row_sum = sums[0]
        row_scale = 1.0 / row_sum

    target_sum = scaled_product(sink_weight, row_scale, swapped)
    summed = proto_total * (soft_sum - column_factor * target_sum)

    square_mean = jnp.mean(raw_rows * raw_rows, axis=1, keepdims=True)
    factor = lax.rsqrt(embed_width * (square_mean + 1e-06))
    inner_prod = jnp.sum(raw_rows * summed, axis=1, keepdims=True)
    gradient = factor * summed - factor * raw_rows * inner_prod / (
        embed_width * (square_mean + 1e-06)
    )
    out_scale = embed_width / math.sqrt(crops)
    own_gradient = (out_scale * gradient).astype(jnp.bfloat16)
    return gather_rows(own_gradient)


def solution(mesh):
    return jax.shard_map(
        shards,
        mesh=mesh,
        in_specs=(
            P(("row", "col"), None),
            P(None, "tp"),
            P("tp", None),
            P(),
            P(("col", "tp"), None),
            P("row"),
        ),
        out_specs=P(("col", "tp"), None),
        check_vma=False,
    )
```

```python
import functools
import math

import jax
import jax.numpy as jnp
from jax import lax
from jax.experimental import pallas as pl
from jax.experimental.pallas import tpu as pltpu
from jax.sharding import PartitionSpec as P

ITERS = 3


SOFTMAX_TEMPER = 0.1
LOG2_E = 1.4426950408889634
CROP_STEP = 512
PROTO_STEP = 256
BALANCE_STEP = 128
ROW_STEP = 2048


def unit_rows(matrix):
    square_mean = jnp.mean(matrix * matrix, axis=-1, keepdims=True)
    return matrix * lax.rsqrt(matrix.shape[-1] * (square_mean + 1e-06))


def shifted(block, axis, target):
    count = lax.axis_size(axis)
    return lax.ppermute(block, axis, [(device, target(device) % count) for device in range(count)])


def placed(pieces, count):
    rows = pieces[0][0].shape
    result = jnp.zeros((count,) + rows, pieces[0][0].dtype)
    for piece, place in pieces:
        result = lax.dynamic_update_slice_in_dim(result, piece[None], place, 0)
    return result


def pairwise_sum(block, axis):
    count = lax.axis_size(axis)
    terms = [block] + [
        shifted(block, axis, lambda device, step=step: device ^ step) for step in range(1, count)
    ]
    while len(terms) > 1:
        terms = [terms[at] + terms[at + 1] for at in range(0, len(terms), 2)]
    return terms[0]


def broadcast_along(block, axes):
    count = lax.axis_size(axes)
    copies = jnp.broadcast_to(block, (count,) + block.shape)
    return lax.all_to_all(copies, axes, 0, 0, tiled=True)


def together(*values):
    return lax.optimization_barrier(values)


def total_sum(parts, beside=None, inputs=()):
    count, crops = parts.shape
    cols = lax.axis_size("col")
    share = crops // cols
    scattered = jnp.swapaxes(parts.reshape(count, cols, share), 0, 1).reshape(cols, count * share)
    own = jnp.sum(lax.all_to_all(scattered, "col", 0, 0, tiled=True), axis=0)
    if count > 1:
        own = own.astype(jnp.bfloat16)
    result = None
    if beside is not None:
        own, *inputs = together(own, *inputs)
    terms = broadcast_along(own, ("row", "tp"))
    if beside is not None:
        terms, result = together(terms, beside(*inputs))
    own = jnp.sum(terms.astype(jnp.float32), axis=0)
    gathered = broadcast_along(own, "col").reshape(cols, count, share)
    return jnp.swapaxes(gathered, 0, 1).reshape(count, crops), result


def gather_embeddings(local_embed, weigh, beside):
    row, col = lax.axis_index("row"), lax.axis_index("col")
    far = shifted(local_embed, "row", lambda device: device ^ 1)
    pair = placed([(local_embed, row % 2), (far, 1 - row % 2)], 2)
    line = [
        (pair, row // 2),
        (shifted(pair, "row", lambda device: device + 2), (row // 2 + 3) % 4),
        (shifted(pair, "row", lambda device: device - 2), (row // 2 + 1) % 4),
        (shifted(pair, "row", lambda device: device + 4), (row // 2 + 2) % 4),
    ]
    block = placed(line, 4).reshape(-1, local_embed.shape[1])
    swap = lambda piece: shifted(piece, "col", lambda device: device ^ 1)
    others = [
        ((col + 6) % 8, shifted(block, "col", lambda device: device + 2)),
        ((col + 2) % 8, shifted(block, "col", lambda device: device - 2)),
        ((col + 4) % 8, shifted(block, "col", lambda device: device + 4)),
    ]
    twin = swap(block)
    weights = weigh(col, block, [])
    weights = weigh(col ^ 1, twin, weights)
    places = [place for place, _ in others]
    *pieces, beside, weights[2] = together(*[piece for _, piece in others], beside, weights[2])
    twins = [swap(piece) for piece in pieces]
    for place, piece, twin in zip(places, pieces, twins):
        weights = weigh(place, piece, weights)
        weights = weigh(place ^ 1, twin, weights)
    return weights, beside


def first_kernel(place_ref, own_ref, out_ref):
    out_ref[0] = own_ref[...]


def first_placed(own, place, count):
    rows, width = own.shape
    return pl.pallas_call(
        first_kernel,
        grid_spec=pltpu.PrefetchScalarGridSpec(
            num_scalar_prefetch=1,
            grid=(1,),
            in_specs=[pl.BlockSpec((rows, width), lambda at, place: (0, 0))],
            out_specs=pl.BlockSpec((1, rows, width), lambda at, place: (place[0], 0, 0)),
        ),
        out_shape=jax.ShapeDtypeStruct((count, rows, width), own.dtype),
        name="first_placed",
    )(place.reshape(1).astype(jnp.int32), own)


def gather_rows(own):
    row = lax.axis_index("row")
    half = own.shape[0] // 2
    quarter = half // 2
    over = row ^ 1
    flip = lambda block: shifted(block, "row", lambda device: device ^ 1)
    right = lambda block: shifted(block, "row", lambda device: device + 2)
    left = lambda block: shifted(block, "row", lambda device: device - 2)
    first, second = own[:half], own[half:]
    own, first, second = together(own, first, second)
    far0, far1 = flip(first), flip(second)
    result = first_placed(own, row, 8)
    own, result = together(own, result)
    near_r, near_l = right(own), left(own)

    def put(result, piece, place, start):
        return lax.dynamic_update_slice(result, piece[None], (place & 7, start, 0))

    far0, near_r, near_l = together(far0, near_r, near_l)
    opp_r, opp_l = right(near_r[:half]), left(near_l[half:])
    far0_r, far0_l = right(far0), left(far0)
    result = put(result, near_r, row + 6, 0)
    result = put(result, near_l, row + 2, 0)
    result = put(result, far0, over, 0)
    result, far1, opp_r, opp_l, far0_r, far0_l = together(
        result, far1, opp_r, opp_l, far0_r, far0_l
    )
    far1_r, far1_l = right(far1), left(far1)
    far0_or, far0_ol = right(far0_r[:quarter]), left(far0_l[quarter:])
    result = put(result, opp_r, row + 4, 0)
    result = put(result, opp_l, row + 4, half)
    result = put(result, far0_r, over + 6, 0)
    result = put(result, far0_l, over + 2, 0)
    result = put(result, far1, over, half)
    result, far1_r, far1_l, far0_or, far0_ol = together(result, far1_r, far1_l, far0_or, far0_ol)
    far1_or, far1_ol = right(far1_r[:quarter]), left(far1_l[quarter:])
    result = put(result, far0_or, over + 4, 0)
    result = put(result, far0_ol, over + 4, quarter)
    result = put(result, far1_r, over + 6, half)
    result = put(result, far1_l, over + 2, half)
    result, far1_or, far1_ol = together(result, far1_or, far1_ol)
    result = put(result, far1_or, over + 4, half)
    result = put(result, far1_ol, over + 4, half + quarter)
    return result.reshape(-1, own.shape[1])


def weights_kernel(place_ref, protos_ref, embed_ref, *refs):
    sink_ref, soft_ref, total_ref, copy_ref = refs[-4:]
    embed = embed_ref[...]
    copy_ref[...] = embed
    total = jnp.zeros((1, embed.shape[0]), jnp.float32)
    for start in range(0, protos_ref.shape[0], PROTO_STEP):
        rows = pl.ds(start, PROTO_STEP)
        score = lax.dot_general(
            protos_ref[rows, :], embed, (((1,), (1,)), ((), ())), preferred_element_type=jnp.float32
        )
        weight = jnp.exp2(score * (LOG2_E / SOFTMAX_TEMPER))
        soft_ref[rows, :] = weight.astype(jnp.bfloat16)
        sink_ref[rows, :] = (weight * weight).astype(jnp.bfloat16)
        total += jnp.sum(weight, axis=0, keepdims=True)
    total_ref[...] = total


def exp_weights(place, protos, block, crops, before):
    count, width = protos.shape
    step = CROP_STEP
    steps = block.shape[0] // step
    shapes = [
        jax.ShapeDtypeStruct((count, crops), jnp.bfloat16),
        jax.ShapeDtypeStruct((count, crops), jnp.bfloat16),
        jax.ShapeDtypeStruct((1, crops), jnp.float32),
        jax.ShapeDtypeStruct((crops, width), jnp.bfloat16),
    ]
    return pl.pallas_call(
        weights_kernel,
        grid_spec=pltpu.PrefetchScalarGridSpec(
            num_scalar_prefetch=1,
            grid=(steps,),
            in_specs=[
                pl.BlockSpec((count, width), lambda at, place: (0, 0)),
                pl.BlockSpec((step, width), lambda at, place: (at, 0)),
            ]
            + [pl.BlockSpec(memory_space=pl.ANY)] * len(before),
            out_specs=[
                pl.BlockSpec((count, step), lambda at, place: (0, place[0] * steps + at)),
                pl.BlockSpec((count, step), lambda at, place: (0, place[0] * steps + at)),
                pl.BlockSpec((1, step), lambda at, place: (0, place[0] * steps + at)),
                pl.BlockSpec((step, width), lambda at, place: (place[0] * steps + at, 0)),
            ],
        ),
        out_shape=shapes,
        input_output_aliases={3 + at: at for at in range(len(before))},
        compiler_params=pltpu.CompilerParams(vmem_limit_bytes=60 << 20),
        cost_estimate=pl.CostEstimate(
            flops=2 * count * block.shape[0] * width,
            bytes_accessed=8 * count * block.shape[0],
            transcendentals=count * block.shape[0],
        ),
        name="exp_weights",
    )(place.reshape(1).astype(jnp.int32), protos, block, *before)


def start_copies(source, held, landed, rows):
    copies = []
    for at in range(0, source.shape[0], rows):
        span = pl.ds(at, rows)
        copies.append(
            pltpu.make_async_copy(source.at[span], held.at[span], landed.at[at // rows])
        )
        copies[-1].start()
    return copies


def balance_kernel(scale_ref, sink_hbm, row_ref, column_ref, held, landed):
    count, crops = held.shape
    rows, lanes, stride = BALANCE_STEP, 128, 2048
    copies = start_copies(sink_hbm, held, landed, rows)
    for at in range(0, count, rows):
        copies[at // rows].wait()
        span = pl.ds(at, rows)
        part = jnp.zeros((rows, lanes), jnp.float32)
        for start in range(0, crops, lanes):
            columns = pl.ds(start, lanes)
            part += held[span, columns].astype(jnp.float32) * scale_ref[:, columns]
        column = 1.0 / jnp.sum(part, axis=1, keepdims=True)
        column_ref[span, :] = column
        across = jnp.broadcast_to(column, (rows, lanes)).T[:8, :]
        high = across.astype(jnp.bfloat16)
        low = (across - high.astype(jnp.float32)).astype(jnp.bfloat16)
        both = jnp.concatenate([high, low], axis=0)
        for start in range(0, crops, stride):
            columns = pl.ds(start, stride)
            product = jnp.dot(both, held[span, columns], preferred_element_type=jnp.float32)
            product = product[0:1, :] + product[8:9, :]
            if at == 0:
                row_ref[:, columns] = product
            else:
                row_ref[:, columns] += product


def balance(row_scale, sink_weight):
    count, crops = sink_weight.shape
    vmem = pl.BlockSpec(memory_space=pltpu.VMEM)
    return pl.pallas_call(
        balance_kernel,
        in_specs=[vmem, pl.BlockSpec(memory_space=pl.ANY)],
        out_specs=[vmem, vmem],
        out_shape=[
            jax.ShapeDtypeStruct((1, crops), jnp.float32),
            jax.ShapeDtypeStruct((count, 1), jnp.float32),
        ],
        scratch_shapes=[
            pltpu.VMEM((count, crops), jnp.bfloat16),
            pltpu.SemaphoreType.DMA((count // BALANCE_STEP,)),
        ],
        compiler_params=pltpu.CompilerParams(vmem_limit_bytes=56 << 20),
        cost_estimate=pl.CostEstimate(
            flops=4 * count * crops, bytes_accessed=2 * count * crops, transcendentals=0
        ),
        name="balance",
    )(row_scale.reshape(1, crops), sink_weight)


def product_kernel(scale_ref, rows_hbm, weight_hbm, out_ref, scaled, held, landed, landed_rows):
    lanes = 128
    count, crops = held.shape
    row_copies = start_copies(rows_hbm, scaled, landed_rows, ROW_STEP)
    copies = start_copies(weight_hbm, held, landed, PROTO_STEP)
    for start in range(0, crops, lanes):
        if start % ROW_STEP == 0:
            row_copies[start // ROW_STEP].wait()
        span = pl.ds(start, lanes)
        scale = jnp.broadcast_to(scale_ref[:, span], (lanes, lanes)).T
        for at in range(0, scaled.shape[1], lanes):
            columns = pl.ds(at, lanes)
            values = scaled[span, columns].astype(jnp.float32) * scale
            scaled[span, columns] = values.astype(jnp.bfloat16)
    for start in range(0, count, PROTO_STEP):
        copies[start // PROTO_STEP].wait()
        protos = pl.ds(start, PROTO_STEP)
        out_ref[protos, :] = jnp.dot(
            held[protos, :], scaled[...], preferred_element_type=jnp.float32
        )


def scaled_product(weight, scale, rows):
    count, crops = weight.shape
    width = rows.shape[1]
    vmem, anywhere = pl.BlockSpec(memory_space=pltpu.VMEM), pl.BlockSpec(memory_space=pl.ANY)
    return pl.pallas_call(
        product_kernel,
        in_specs=[vmem, anywhere, anywhere],
        out_specs=vmem,
        out_shape=jax.ShapeDtypeStruct((count, width), jnp.float32),
        scratch_shapes=[
            pltpu.VMEM((crops, width), jnp.bfloat16),
            pltpu.VMEM((count, crops), jnp.bfloat16),
            pltpu.SemaphoreType.DMA((count // PROTO_STEP,)),
            pltpu.SemaphoreType.DMA((crops // ROW_STEP,)),
        ],
        compiler_params=pltpu.CompilerParams(vmem_limit_bytes=56 << 20),
        cost_estimate=pl.CostEstimate(
            flops=2 * count * crops * width,
            bytes_accessed=2 * count * crops + 2 * crops * width,
            transcendentals=0,
        ),
        name="scaled_product",
    )(scale.reshape(1, crops), rows, weight)


def swap_kernel(partner_ref, embed_ref, out_ref):
    cols, _, share, width = embed_ref.shape
    rows = cols * share
    place = lax.broadcasted_iota(jnp.int32, (rows, rows), 0)
    chosen = jnp.where(place == partner_ref[0], 1.0, 0.0).astype(jnp.bfloat16)
    embed = embed_ref[...].reshape(rows, width)
    swapped = jnp.dot(chosen, embed, preferred_element_type=jnp.float32)
    out_ref[...] = swapped.astype(jnp.bfloat16).reshape(embed_ref.shape)


def swap_partners(local_partner, embedding):
    blocks, rows = local_partner.shape
    width = embedding.shape[1]
    cols = lax.axis_size("col")
    split = (cols, blocks, rows // cols, width)
    spec = pl.BlockSpec((cols, 1, rows // cols, width), lambda at: (0, at, 0, 0))
    return pl.pallas_call(
        swap_kernel,
        grid=(blocks,),
        in_specs=[pl.BlockSpec((1, 1, rows), lambda at: (at, 0, 0)), spec],
        out_specs=spec,
        out_shape=jax.ShapeDtypeStruct(split, jnp.bfloat16),
        compiler_params=pltpu.CompilerParams(vmem_limit_bytes=60 << 20),
        cost_estimate=pl.CostEstimate(
            flops=2 * blocks * rows * rows * width,
            bytes_accessed=16 * blocks * rows * width,
            transcendentals=0,
        ),
        name="swap_partners",
    )(local_partner.reshape(blocks, 1, rows), embedding.reshape(split)).reshape(embedding.shape)


def shards(crop_rows, up_weight, down_weight, proj_weight, prototypes, partner):
    tp_count = lax.axis_size("tp")
    col_count = lax.axis_size("col")
    row_count = lax.axis_size("row")
    crop_values = crop_rows.astype(jnp.float32)
    centred = crop_values - jnp.mean(crop_values, axis=1, keepdims=True)
    normed = (
        centred * lax.rsqrt(jnp.mean(centred * centred, axis=1, keepdims=True) + 1e-05)
    ).astype(jnp.bfloat16)
    hidden = jax.nn.gelu(jnp.dot(normed, up_weight, preferred_element_type=jnp.float32)).astype(
        jnp.bfloat16
    )
    branch_out = jnp.dot(hidden, down_weight, preferred_element_type=jnp.float32)
    partial_proj = jnp.dot(
        crop_values / tp_count + branch_out,
        proj_weight.astype(jnp.float32),
        precision=lax.Precision.HIGHEST,
    )
    embed_width = partial_proj.shape[1]
    block_rows = partner.shape[0]
    proto_total = prototypes.shape[0] * col_count * tp_count
    own_count = prototypes.shape[0] // row_count
    own_rows = lax.dynamic_slice_in_dim(
        prototypes, lax.axis_index("row") * own_count, own_count, 0
    )
    raw_rows = own_rows.astype(jnp.float32)
    unit_protos = unit_rows(raw_rows).astype(jnp.bfloat16)

    local_raw, unit_protos = together(pairwise_sum(partial_proj, "tp"), unit_protos)
    local_embed = unit_rows(local_raw).astype(jnp.bfloat16)

    crops = row_count * block_rows
    weights, partners = gather_embeddings(
        local_embed,
        lambda place, block, before: list(exp_weights(place, unit_protos, block, crops, before)),
        broadcast_along(partner, "row"),
    )
    partners = partners.reshape(row_count, block_rows)
    local_partner = partners - block_rows * jnp.arange(row_count, dtype=jnp.int32)[:, None]
    sink_weight, soft_weight, soft_part, embedding = weights
    row_scale = jnp.ones((crops,), jnp.float32)
    for iteration in range(ITERS):
        row_part, column_factor = balance(row_scale, sink_weight)
        if iteration == 0:
            sums, _ = total_sum(jnp.concatenate([row_part, soft_part], axis=0))
            row_sum, soft_scale = sums[0], 1.0 / sums[1]
        elif iteration == 1:
            sums, soft_sum = total_sum(
                row_part, scaled_product, (soft_weight, soft_scale, embedding)
            )
            row_sum = sums[0]
        else:
            sums, swapped = total_sum(row_part, swap_partners, (local_partner, embedding))
            row_sum = sums[0]
        row_scale = 1.0 / row_sum

    target_sum = scaled_product(sink_weight, row_scale, swapped)
    summed = proto_total * (soft_sum - column_factor * target_sum)

    square_mean = jnp.mean(raw_rows * raw_rows, axis=1, keepdims=True)
    factor = lax.rsqrt(embed_width * (square_mean + 1e-06))
    inner_prod = jnp.sum(raw_rows * summed, axis=1, keepdims=True)
    gradient = factor * summed - factor * raw_rows * inner_prod / (
        embed_width * (square_mean + 1e-06)
    )
    out_scale = embed_width / math.sqrt(crops)
    own_gradient = (out_scale * gradient).astype(jnp.bfloat16)
    return gather_rows(own_gradient)


def solution(mesh):
    return jax.shard_map(
        shards,
        mesh=mesh,
        in_specs=(
            P(("row", "col"), None),
            P(None, "tp"),
            P("tp", None),
            P(),
            P(("col", "tp"), None),
            P("row"),
        ),
        out_specs=P(("col", "tp"), None),
        check_vma=False,
    )
```

```python
import functools
import math

import jax
import jax.numpy as jnp
from jax import lax
from jax.experimental import pallas as pl
from jax.experimental.pallas import tpu as pltpu
from jax.sharding import PartitionSpec as P

ITERS = 3


SOFTMAX_TEMPER = 0.1
LOG2_E = 1.4426950408889634
CROP_STEP = 256
PROTO_STEP = 256
BALANCE_STEP = 128
PRODUCT_STEP = 256
ROW_STEP = 2048
CODE_ROWS = 16
CODE_BASE = 32


def unit_rows(matrix):
    square_mean = jnp.mean(matrix * matrix, axis=-1, keepdims=True)
    return matrix * lax.rsqrt(matrix.shape[-1] * (square_mean + 1e-06))


def shifted(block, axis, target):
    count = lax.axis_size(axis)
    return lax.ppermute(block, axis, [(device, target(device) % count) for device in range(count)])


def placed(pieces, count):
    rows = pieces[0][0].shape
    result = jnp.zeros((count,) + rows, pieces[0][0].dtype)
    for piece, place in pieces:
        result = lax.dynamic_update_slice_in_dim(result, piece[None], place, 0)
    return result


def pairwise_sum(block, axis):
    count = lax.axis_size(axis)
    terms = [block] + [
        shifted(block, axis, lambda device, step=step: device ^ step) for step in range(1, count)
    ]
    while len(terms) > 1:
        terms = [terms[at] + terms[at + 1] for at in range(0, len(terms), 2)]
    return terms[0]


def broadcast_along(block, axes):
    count = lax.axis_size(axes)
    copies = jnp.broadcast_to(block, (count,) + block.shape)
    return lax.all_to_all(copies, axes, 0, 0, tiled=True)


def together(*values):
    return lax.optimization_barrier(values)


def total_sum(parts, beside=None, inputs=()):
    count, lines, lanes = parts.shape
    cols = lax.axis_size("col")
    share = lines // cols
    scattered = jnp.swapaxes(parts.reshape(count, cols, share, lanes), 0, 1)
    own = jnp.sum(lax.all_to_all(scattered, "col", 0, 0, tiled=True), axis=0)
    if count > 1:
        own = own.astype(jnp.bfloat16)
    result = None
    if beside is not None:
        own, *inputs = together(own, *inputs)
    terms = broadcast_along(own.reshape(-1, lanes), ("row", "tp"))
    if beside is not None:
        terms, result = together(terms, beside(*inputs))
    own = jnp.sum(terms.astype(jnp.float32), axis=0)
    gathered = broadcast_along(own, "col").reshape(cols, count, share, lanes)
    return jnp.swapaxes(gathered, 0, 1).reshape(count, lines, lanes), result


def gather_embeddings(local_embed, weigh):
    row, col = lax.axis_index("row"), lax.axis_index("col")
    far = shifted(local_embed, "row", lambda device: device ^ 1)
    pair = placed([(local_embed, row % 2), (far, 1 - row % 2)], 2)
    line = [
        (pair, row // 2),
        (shifted(pair, "row", lambda device: device + 2), (row // 2 + 3) % 4),
        (shifted(pair, "row", lambda device: device - 2), (row // 2 + 1) % 4),
        (shifted(pair, "row", lambda device: device + 4), (row // 2 + 2) % 4),
    ]
    block = placed(line, 4).reshape((-1,) + local_embed.shape)
    swap = lambda piece: shifted(piece, "col", lambda device: device ^ 1)
    others = [
        ((col + 6) % 8, shifted(block, "col", lambda device: device + 2)),
        ((col + 2) % 8, shifted(block, "col", lambda device: device - 2)),
        ((col + 4) % 8, shifted(block, "col", lambda device: device + 4)),
    ]
    twin = swap(block)
    weights = weigh(col, block, [])
    weights = weigh(col ^ 1, twin, weights)
    places = [place for place, _ in others]
    *pieces, weights[2] = together(*[piece for _, piece in others], weights[2])
    twins = [swap(piece) for piece in pieces]
    for place, piece, twin in zip(places, pieces, twins):
        weights = weigh(place, piece, weights)
        weights = weigh(place ^ 1, twin, weights)
    return weights


def first_kernel(place_ref, own_ref, out_ref):
    out_ref[0] = own_ref[...]


def first_placed(own, place, shape):
    rows, width = own.shape
    return pl.pallas_call(
        first_kernel,
        grid_spec=pltpu.PrefetchScalarGridSpec(
            num_scalar_prefetch=1,
            grid=(1,),
            in_specs=[pl.BlockSpec((rows, width), lambda at, place: (0, 0))],
            out_specs=pl.BlockSpec((1, rows, width), lambda at, place: (place[0], 0, 0)),
        ),
        out_shape=jax.ShapeDtypeStruct(shape, own.dtype),
        name="first_placed",
    )(place.reshape(1).astype(jnp.int32), own)


def gather_rows(own0, own1):
    row = lax.axis_index("row")
    half, width = own0.shape
    quarter = half // 2
    over = row ^ 1
    flip = lambda block: shifted(block, "row", lambda device: device ^ 1)
    right = lambda block: shifted(block, "row", lambda device: device + 2)
    left = lambda block: shifted(block, "row", lambda device: device - 2)

    def put(result, piece, place, start):
        return lax.dynamic_update_slice(result, piece[None], (place & 7, start, 0))

    far0, near0_r, near0_l = flip(own0), right(own0), left(own0)
    far1, near1_r, near1_l = flip(own1), right(own1), left(own1)
    result = first_placed(own0, row, (8, 2 * half, width))
    result = put(result, own1, row, half)
    result, far0, near0_r, near0_l, near1_r, near1_l = together(
        result, far0, near0_r, near0_l, near1_r, near1_l
    )
    far0_r, far0_l, opp0, opp1 = right(far0), left(far0), right(near0_r), left(near1_l)
    result = put(result, near0_r, row + 6, 0)
    result = put(result, near0_l, row + 2, 0)
    result = put(result, far0, over, 0)
    result = put(result, near1_r, row + 6, half)
    result = put(result, near1_l, row + 2, half)
    result, far1, far0_r, far0_l, opp0, opp1 = together(result, far1, far0_r, far0_l, opp0, opp1)
    far1_r, far1_l = right(far1), left(far1)
    far0_or, far0_ol = right(far0_r[:quarter]), left(far0_l[quarter:])
    result = put(result, opp0, row + 4, 0)
    result = put(result, opp1, row + 4, half)
    result = put(result, far0_r, over + 6, 0)
    result = put(result, far0_l, over + 2, 0)
    result = put(result, far1, over, half)
    result, far1_r, far1_l, far0_or, far0_ol = together(result, far1_r, far1_l, far0_or, far0_ol)
    far1_or, far1_ol = right(far1_r[:quarter]), left(far1_l[quarter:])
    result = put(result, far0_or, over + 4, 0)
    result = put(result, far0_ol, over + 4, quarter)
    result = put(result, far1_r, over + 6, half)
    result = put(result, far1_l, over + 2, half)
    result, far1_or, far1_ol = together(result, far1_or, far1_ol)
    result = put(result, far1_or, over + 4, half)
    result = put(result, far1_ol, over + 4, half + quarter)
    return result.reshape(-1, width)


def weights_kernel(place_ref, protos_ref, embed_ref, *refs):
    sink_ref, soft_ref, total_ref, copy_ref, code_ref = refs[-5:]
    step, width = copy_ref.shape
    share = embed_ref.shape[1] - CODE_ROWS
    embed = embed_ref[:, :share, :].reshape(step, width)
    copy_ref[...] = embed
    code_ref[0] = embed_ref[:, share:, :]
    total = jnp.zeros((1, step), jnp.float32)
    for start in range(0, protos_ref.shape[0], PROTO_STEP):
        rows = pl.ds(start, PROTO_STEP)
        score = lax.dot_general(
            protos_ref[rows, :], embed, (((1,), (1,)), ((), ())), preferred_element_type=jnp.float32
        )
        weight = jnp.exp2(score * (LOG2_E / SOFTMAX_TEMPER))
        soft_ref[rows, :] = weight.astype(jnp.bfloat16)
        sink_ref[rows, :] = (weight * weight).astype(jnp.bfloat16)
        total += jnp.sum(weight, axis=0, keepdims=True)
    lines = step // 128
    for line in range(lines):
        total_ref[pl.ds(pl.program_id(0) * lines + line, 1), :] = total[
            :, line * 128 : (line + 1) * 128
        ]


def exp_weights(place, protos, block, before):
    count, width = protos.shape
    groups, share, _ = block.shape
    share -= CODE_ROWS
    per_step = CROP_STEP // share
    steps = groups // per_step
    blocks = lax.axis_size("col")
    crops = blocks * groups * share
    spread = lambda at, place: (0, place[0] * steps + at)
    return pl.pallas_call(
        weights_kernel,
        grid_spec=pltpu.PrefetchScalarGridSpec(
            num_scalar_prefetch=1,
            grid=(steps,),
            in_specs=[
                pl.BlockSpec((count, width), lambda at, place: (0, 0)),
                pl.BlockSpec((per_step, share + CODE_ROWS, width), lambda at, place: (at, 0, 0)),
            ]
            + [pl.BlockSpec(memory_space=pl.ANY)] * len(before),
            out_specs=[
                pl.BlockSpec((count, CROP_STEP), spread),
                pl.BlockSpec((count, CROP_STEP), spread),
                pl.BlockSpec((groups * share // 128, 128), lambda at, place: (place[0], 0)),
                pl.BlockSpec((CROP_STEP, width), lambda at, place: (place[0] * steps + at, 0)),
                pl.BlockSpec((1, per_step, CODE_ROWS, width), lambda at, place: (place[0], at, 0, 0)),
            ],
        ),
        out_shape=[
            jax.ShapeDtypeStruct((count, crops), jnp.bfloat16),
            jax.ShapeDtypeStruct((count, crops), jnp.bfloat16),
            jax.ShapeDtypeStruct((crops // 128, 128), jnp.float32),
            jax.ShapeDtypeStruct((crops, width), jnp.bfloat16),
            jax.ShapeDtypeStruct((blocks, groups, CODE_ROWS, width), jnp.bfloat16),
        ],
        input_output_aliases={3 + at: at for at in range(len(before))},
        compiler_params=pltpu.CompilerParams(vmem_limit_bytes=59 << 20),
        cost_estimate=pl.CostEstimate(
            flops=2 * count * groups * share * width,
            bytes_accessed=8 * count * groups * share,
            transcendentals=count * groups * share,
        ),
        name="exp_weights",
    )(place.reshape(1).astype(jnp.int32), protos, block, *before)


class Copies:
    def __init__(self, source, held, landed, rows, first=0):
        self.parts = []
        for at in range(held.shape[0] // rows):
            self.parts.append(
                pltpu.make_async_copy(
                    source.at[pl.ds(first + at * rows, rows)],
                    held.at[pl.ds(at * rows, rows)],
                    landed.at[at],
                )
            )

    def start(self, at):
        if at < len(self.parts):
            self.parts[at].start()

    def wait(self, at):
        self.parts[at].wait()
        self.start(at + 2)


def balance_kernel(scale_ref, sink_hbm, row_ref, column_ref, held, sums, landed):
    count, crops = held.shape
    rows, lanes, stride = BALANCE_STEP, 128, 2048
    copies = Copies(sink_hbm, held, landed, rows)
    copies.start(0)
    copies.start(1)
    for at in range(0, count, rows):
        copies.wait(at // rows)
        span = pl.ds(at, rows)
        part = jnp.zeros((rows, lanes), jnp.float32)
        for line in range(crops // lanes):
            values = held[span, pl.ds(line * lanes, lanes)].astype(jnp.float32)
            part += values * scale_ref[pl.ds(line, 1), :]
        column = 1.0 / jnp.sum(part, axis=1, keepdims=True)
        column_ref[span, :] = column
        across = jnp.broadcast_to(column, (rows, lanes)).T[:8, :]
        high = across.astype(jnp.bfloat16)
        low = (across - high.astype(jnp.float32)).astype(jnp.bfloat16)
        both = jnp.concatenate([high, low], axis=0)
        for start in range(0, crops, stride):
            columns = pl.ds(start, stride)
            product = jnp.dot(both, held[span, columns], preferred_element_type=jnp.float32)
            product = product[0:1, :] + product[8:9, :]
            if at == 0:
                sums[:, columns] = product
            else:
                sums[:, columns] += product
    for line in range(crops // lanes):
        row_ref[pl.ds(line, 1), :] = sums[:, pl.ds(line * lanes, lanes)]


def balance(row_scale, sink_weight):
    count, crops = sink_weight.shape
    vmem = pl.BlockSpec(memory_space=pltpu.VMEM)
    return pl.pallas_call(
        balance_kernel,
        in_specs=[vmem, pl.BlockSpec(memory_space=pl.ANY)],
        out_specs=[vmem, vmem],
        out_shape=[
            jax.ShapeDtypeStruct(row_scale.shape, jnp.float32),
            jax.ShapeDtypeStruct((count, 1), jnp.float32),
        ],
        scratch_shapes=[
            pltpu.VMEM((count, crops), jnp.bfloat16),
            pltpu.VMEM((1, crops), jnp.float32),
            pltpu.SemaphoreType.DMA((count // BALANCE_STEP,)),
        ],
        compiler_params=pltpu.CompilerParams(vmem_limit_bytes=56 << 20),
        cost_estimate=pl.CostEstimate(
            flops=4 * count * crops, bytes_accessed=2 * count * crops, transcendentals=0
        ),
        name="balance",
    )(row_scale, sink_weight)


def product_kernel(first, finish, scale_ref, rows_hbm, weight_hbm, *refs):
    *extra, out_ref, scaled, held, landed, landed_rows = refs
    lanes = 128
    count, crops = held.shape
    row_copies = Copies(rows_hbm, scaled, landed_rows, ROW_STEP)
    copies = Copies(weight_hbm, held, landed, PRODUCT_STEP, first)
    row_copies.start(0)
    row_copies.start(1)
    for line in range(crops // lanes):
        if line * lanes % ROW_STEP == 0:
            at = line * lanes // ROW_STEP
            row_copies.wait(at)
            if at >= len(row_copies.parts) - 2:
                copies.start(at - len(row_copies.parts) + 2)
        span = pl.ds(line * lanes, lanes)
        scale = jnp.broadcast_to(scale_ref[pl.ds(line, 1), :], (lanes, lanes)).T
        for at in range(0, scaled.shape[1], lanes):
            columns = pl.ds(at, lanes)
            values = scaled[span, columns].astype(jnp.float32) * scale
            scaled[span, columns] = values.astype(jnp.bfloat16)
    for start in range(0, count, PRODUCT_STEP):
        copies.wait(start // PRODUCT_STEP)
        protos = pl.ds(start, PRODUCT_STEP)
        product = jnp.dot(held[protos, :], scaled[...], preferred_element_type=jnp.float32)
        if finish is not None:
            own = pl.ds(first + start, PRODUCT_STEP)
            product = finish(product, *[ref[own, :] for ref in extra])
        out_ref[protos, :] = product.astype(out_ref.dtype)


def scaled_product(weight, scale, rows, first=0, count=None, finish=None, extra=(), kind=jnp.float32):
    crops = weight.shape[1]
    count = weight.shape[0] if count is None else count
    width = rows.shape[1]
    vmem, anywhere = pl.BlockSpec(memory_space=pltpu.VMEM), pl.BlockSpec(memory_space=pl.ANY)
    return pl.pallas_call(
        functools.partial(product_kernel, first, finish),
        in_specs=[vmem, anywhere, anywhere] + [vmem] * len(extra),
        out_specs=vmem,
        out_shape=jax.ShapeDtypeStruct((count, width), kind),
        scratch_shapes=[
            pltpu.VMEM((crops, width), jnp.bfloat16),
            pltpu.VMEM((count, crops), jnp.bfloat16),
            pltpu.SemaphoreType.DMA((count // PRODUCT_STEP,)),
            pltpu.SemaphoreType.DMA((crops // ROW_STEP,)),
        ],
        compiler_params=pltpu.CompilerParams(vmem_limit_bytes=56 << 20),
        cost_estimate=pl.CostEstimate(
            flops=2 * count * crops * width,
            bytes_accessed=2 * count * crops + 2 * crops * width,
            transcendentals=0,
        ),
        name="scaled_product",
    )(scale, rows, weight, *extra)


def swap_kernel(partner_ref, embed_ref, out_ref):
    cols, _, share, width = embed_ref.shape
    rows = cols * share
    place = lax.broadcasted_iota(jnp.int32, (rows, rows), 0)
    chosen = jnp.where(place == partner_ref[0], 1.0, 0.0).astype(jnp.bfloat16)
    embed = embed_ref[...].reshape(rows, width)
    swapped = jnp.dot(chosen, embed, preferred_element_type=jnp.float32)
    out_ref[...] = swapped.astype(jnp.bfloat16).reshape(embed_ref.shape)


def swap_partners(local_partner, embedding):
    blocks, rows = local_partner.shape
    width = embedding.shape[1]
    cols = lax.axis_size("col")
    split = (cols, blocks, rows // cols, width)
    spec = pl.BlockSpec((cols, 1, rows // cols, width), lambda at: (0, at, 0, 0))
    return pl.pallas_call(
        swap_kernel,
        grid=(blocks,),
        in_specs=[pl.BlockSpec((1, 1, rows), lambda at: (at, 0, 0)), spec],
        out_specs=spec,
        out_shape=jax.ShapeDtypeStruct(split, jnp.bfloat16),
        compiler_params=pltpu.CompilerParams(vmem_limit_bytes=60 << 20),
        cost_estimate=pl.CostEstimate(
            flops=2 * blocks * rows * rows * width,
            bytes_accessed=16 * blocks * rows * width,
            transcendentals=0,
        ),
        name="swap_partners",
    )(local_partner.reshape(blocks, 1, rows), embedding.reshape(split)).reshape(embedding.shape)


def shards(crop_rows, up_weight, down_weight, proj_weight, prototypes, partner):
    tp_count = lax.axis_size("tp")
    col_count = lax.axis_size("col")
    row_count = lax.axis_size("row")
    crop_values = crop_rows.astype(jnp.float32)
    centred = crop_values - jnp.mean(crop_values, axis=1, keepdims=True)
    normed = (
        centred * lax.rsqrt(jnp.mean(centred * centred, axis=1, keepdims=True) + 1e-05)
    ).astype(jnp.bfloat16)
    hidden = jax.nn.gelu(jnp.dot(normed, up_weight, preferred_element_type=jnp.float32)).astype(
        jnp.bfloat16
    )
    branch_out = jnp.dot(hidden, down_weight, preferred_element_type=jnp.float32)
    partial_proj = jnp.dot(
        crop_values / tp_count + branch_out,
        proj_weight.astype(jnp.float32),
        precision=lax.Precision.HIGHEST,
    )
    embed_width = partial_proj.shape[1]
    block_rows = partner.shape[0]
    proto_total = prototypes.shape[0] * col_count * tp_count
    own_count = prototypes.shape[0] // row_count
    own_rows = lax.dynamic_slice_in_dim(
        prototypes, lax.axis_index("row") * own_count, own_count, 0
    )
    raw_rows = own_rows.astype(jnp.float32)
    unit_protos = unit_rows(raw_rows).astype(jnp.bfloat16)

    local_raw, unit_protos = together(pairwise_sum(partial_proj, "tp"), unit_protos)
    local_embed = unit_rows(local_raw).astype(jnp.bfloat16)
    share = local_embed.shape[0]
    own_partner = lax.dynamic_slice_in_dim(partner, lax.axis_index("col") * share, share)
    own_partner = own_partner - block_rows * lax.axis_index("row")
    code = jnp.stack([own_partner // CODE_BASE, own_partner % CODE_BASE]).astype(jnp.bfloat16)
    code = jnp.pad(code.reshape(1, -1), ((0, CODE_ROWS - 1), (0, 0)))
    local_embed = jnp.concatenate([local_embed, code], axis=0)

    crops = row_count * block_rows
    weights = gather_embeddings(
        local_embed,
        lambda place, block, before: list(exp_weights(place, unit_protos, block, before)),
    )
    sink_weight, soft_weight, soft_part, embedding, codes = weights
    codes = codes[:, :, 0, :].reshape(col_count, row_count, 2, share).astype(jnp.int32)
    local_partner = CODE_BASE * codes[:, :, 0, :] + codes[:, :, 1, :]
    local_partner = jnp.swapaxes(local_partner, 0, 1).reshape(row_count, block_rows)
    row_scale = jnp.ones(soft_part.shape, jnp.float32)
    for iteration in range(ITERS):
        row_part, column_factor = balance(row_scale, sink_weight)
        if iteration == 0:
            sums, _ = total_sum(jnp.stack([row_part, soft_part]))
            row_sum, soft_scale = sums[0], 1.0 / sums[1]
        elif iteration == 1:
            sums, soft_sum = total_sum(
                row_part[None], scaled_product, (soft_weight, soft_scale, embedding)
            )
            row_sum = sums[0]
        else:
            sums, swapped = total_sum(row_part[None], swap_partners, (local_partner, embedding))
            row_sum = sums[0]
        row_scale = 1.0 / row_sum

    out_scale = embed_width / math.sqrt(crops)

    def gradient(target_part, soft_part, column, protos):
        raw = protos.astype(jnp.float32)
        summed = proto_total * (soft_part - column * target_part)
        square_mean = jnp.mean(raw * raw, axis=1, keepdims=True)
        factor = lax.rsqrt(embed_width * (square_mean + 1e-06))
        inner_prod = jnp.sum(raw * summed, axis=1, keepdims=True)
        result = factor * summed - factor * raw * inner_prod / (
            embed_width * (square_mean + 1e-06)
        )
        return out_scale * result

    def own_half(first, scale):
        return scaled_product(
            sink_weight,
            scale,
            swapped,
            first,
            own_count // 2,
            gradient,
            (soft_sum, column_factor, own_rows),
            jnp.bfloat16,
        )

    return gather_rows(own_half(0, row_scale), own_half(own_count // 2, row_scale))


def solution(mesh):
    return jax.shard_map(
        shards,
        mesh=mesh,
        in_specs=(
            P(("row", "col"), None),
            P(None, "tp"),
            P("tp", None),
            P(),
            P(("col", "tp"), None),
            P("row"),
        ),
        out_specs=P(("col", "tp"), None),
        check_vma=False,
    )
```

```python
import functools
import math

import jax
import jax.numpy as jnp
from jax import lax
from jax.experimental import pallas as pl
from jax.experimental.pallas import tpu as pltpu
from jax.sharding import PartitionSpec as P

ITERS = 3


SOFTMAX_TEMPER = 0.1
LOG2_E = 1.4426950408889634
CROP_STEP = 512
PROTO_STEP = 256
BALANCE_STEP = 128
PRODUCT_STEP = 256
CODE_ROWS = 16
CODE_BASE = 32


def unit_rows(matrix):
    square_mean = jnp.mean(matrix * matrix, axis=-1, keepdims=True)
    return matrix * lax.rsqrt(matrix.shape[-1] * (square_mean + 1e-06))


def shifted(block, axis, target):
    count = lax.axis_size(axis)
    return lax.ppermute(block, axis, [(device, target(device) % count) for device in range(count)])


def placed(pieces, count):
    rows = pieces[0][0].shape
    result = jnp.zeros((count,) + rows, pieces[0][0].dtype)
    for piece, place in pieces:
        result = lax.dynamic_update_slice_in_dim(result, piece[None], place, 0)
    return result


def pairwise_sum(block, axis):
    count = lax.axis_size(axis)
    terms = [block] + [
        shifted(block, axis, lambda device, step=step: device ^ step) for step in range(1, count)
    ]
    while len(terms) > 1:
        terms = [terms[at] + terms[at + 1] for at in range(0, len(terms), 2)]
    return terms[0]


def together(*values):
    return lax.optimization_barrier(values)


def spread_kernel(terms_ref, out_ref):
    total = jnp.sum(terms_ref[...].astype(jnp.float32), axis=0).astype(out_ref.dtype)
    for at in range(out_ref.shape[0]):
        out_ref[at] = total


def sum_and_copies(terms, count, kind):
    vmem = pl.BlockSpec(memory_space=pltpu.VMEM)
    return pl.pallas_call(
        spread_kernel,
        in_specs=[vmem],
        out_specs=vmem,
        out_shape=jax.ShapeDtypeStruct((count,) + terms.shape[1:], kind),
        compiler_params=pltpu.CompilerParams(vmem_limit_bytes=4 << 20),
        name="sum_and_copies",
    )(terms)


def exchanged(blocks, axes):
    return lax.all_to_all(blocks, axes, 0, 0, tiled=True)


def total_sum(parts):
    count, lines, lanes = parts.shape
    cols, others = lax.axis_size("col"), lax.axis_size(("row", "tp"))
    share = lines // cols
    scattered = jnp.swapaxes(parts.reshape(count, cols, share, lanes), 0, 1)
    scattered = scattered.reshape(cols, count * share, lanes)
    kind = jnp.float32 if count == 1 else jnp.bfloat16
    own = sum_and_copies(exchanged(scattered, "col"), others, kind)
    own = sum_and_copies(exchanged(own, ("row", "tp")), cols, jnp.float32)
    gathered = exchanged(own, "col").reshape(cols, count, share, lanes)
    return jnp.swapaxes(gathered, 0, 1).reshape(count, lines, lanes)


def gather_embeddings(local_embed, places, weigh):
    row = lax.axis_index("row")
    far = shifted(local_embed, "row", lambda device: device ^ 1)
    pair = placed([(local_embed, row & 1), (far, 1 - (row & 1))], 2)
    line = [
        (pair, row >> 1),
        (shifted(pair, "row", lambda device: device + 2), ((row >> 1) + 3) & 3),
        (shifted(pair, "row", lambda device: device - 2), ((row >> 1) + 1) & 3),
        (shifted(pair, "row", lambda device: device + 4), ((row >> 1) + 2) & 3),
    ]
    block = placed(line, 4).reshape((-1,) + local_embed.shape)
    swap = lambda piece: shifted(piece, "col", lambda device: device ^ 1)
    others = [
        shifted(block, "col", lambda device: device + 2),
        shifted(block, "col", lambda device: device - 2),
        shifted(block, "col", lambda device: device + 4),
    ]
    twin = swap(block)
    weights = weigh(places[0], (block, twin), [])
    *pieces, weights[2] = together(*others, weights[2])
    twins = [swap(piece) for piece in pieces]
    for place, piece, twin in zip(places[1:], pieces, twins):
        weights = weigh(place, (piece, twin), weights)
    return weights


def first_kernel(place_ref, own_ref, out_ref):
    out_ref[0] = own_ref[...]


def first_placed(own, place, shape):
    rows, width = own.shape
    return pl.pallas_call(
        first_kernel,
        grid_spec=pltpu.PrefetchScalarGridSpec(
            num_scalar_prefetch=1,
            grid=(1,),
            in_specs=[pl.BlockSpec((rows, width), lambda at, place: (0, 0))],
            out_specs=pl.BlockSpec((1, rows, width), lambda at, place: (place[0], 0, 0)),
        ),
        out_shape=jax.ShapeDtypeStruct(shape, own.dtype),
        name="first_placed",
    )(place.reshape(1).astype(jnp.int32), own)


def gather_rows(own0, own1, places):
    half, width = own0.shape
    quarter = half // 2
    near, over = places[:4], places[4:]
    flip = lambda block: shifted(block, "row", lambda device: device ^ 1)
    right = lambda block: shifted(block, "row", lambda device: device + 2)
    left = lambda block: shifted(block, "row", lambda device: device - 2)

    def put(result, piece, place, start):
        start = jnp.uint32(start)
        return lax.dynamic_update_slice(result, piece[None], (place, start, jnp.uint32(0)))

    far0, near0_r, near0_l = flip(own0), right(own0), left(own0)
    far1, near1_r, near1_l = flip(own1), right(own1), left(own1)
    result = first_placed(own0, near[0], (8, 2 * half, width))
    result = put(result, own1, near[0], half)
    result, far0, near0_r, near0_l, near1_r, near1_l = together(
        result, far0, near0_r, near0_l, near1_r, near1_l
    )
    far0_r, far0_l, opp0, opp1 = right(far0), left(far0), right(near0_r), left(near1_l)
    result = put(result, near0_r, near[3], 0)
    result = put(result, near0_l, near[1], 0)
    result = put(result, far0, over[0], 0)
    result = put(result, near1_r, near[3], half)
    result = put(result, near1_l, near[1], half)
    result, far1, far0_r, far0_l, opp0, opp1 = together(result, far1, far0_r, far0_l, opp0, opp1)
    far1_r, far1_l = right(far1), left(far1)
    far0_or, far0_ol = right(far0_r[:quarter]), left(far0_l[quarter:])
    result = put(result, opp0, near[2], 0)
    result = put(result, opp1, near[2], half)
    result = put(result, far0_r, over[3], 0)
    result = put(result, far0_l, over[1], 0)
    result = put(result, far1, over[0], half)
    result, far1_r, far1_l, far0_or, far0_ol = together(result, far1_r, far1_l, far0_or, far0_ol)
    far1_or, far1_ol = right(far1_r[:quarter]), left(far1_l[quarter:])
    result = put(result, far0_or, over[2], 0)
    result = put(result, far0_ol, over[2], quarter)
    result = put(result, far1_r, over[3], half)
    result = put(result, far1_l, over[1], half)
    result, far1_or, far1_ol = together(result, far1_or, far1_ol)
    result = put(result, far1_or, over[2], half)
    result = put(result, far1_ol, over[2], half + quarter)
    return result.reshape(-1, width)


def weights_kernel(place_ref, protos_ref, *refs):
    sink_ref, soft_ref, total_ref, copy_ref, code_ref = refs[-5:]
    for at in range(place_ref.shape[0]):
        embed_ref = refs[at]
        groups, share, width = embed_ref.shape
        share -= CODE_ROWS
        place = place_ref[at]
        per_step = CROP_STEP // share
        code_ref[pl.ds(place, 1)] = embed_ref[:, share:, :][None]
        for group in range(0, groups, per_step):
            columns = pl.ds(pl.multiple_of((place * groups + group) * share, CROP_STEP), CROP_STEP)
            embed = embed_ref[group : group + per_step, :share, :].reshape(CROP_STEP, width)
            copy_ref[columns, :] = embed
            total = jnp.zeros((1, CROP_STEP), jnp.float32)
            for start in range(0, protos_ref.shape[0], PROTO_STEP):
                rows = pl.ds(start, PROTO_STEP)
                score = lax.dot_general(
                    protos_ref[rows, :],
                    embed,
                    (((1,), (1,)), ((), ())),
                    preferred_element_type=jnp.float32,
                )
                weight = jnp.exp2(score * (LOG2_E / SOFTMAX_TEMPER))
                soft_ref[rows, columns] = weight.astype(jnp.bfloat16)
                sink_ref[rows, columns] = (weight * weight).astype(jnp.bfloat16)
                total += jnp.sum(weight, axis=0, keepdims=True)
            for line in range(per_step):
                total_ref[pl.ds(place * groups + group + line, 1), :] = total[
                    :, line * share : (line + 1) * share
                ]


VMEM_SPEC = pl.BlockSpec(memory_space=pltpu.VMEM)


def exp_weights(places, protos, pieces, before):
    count, width = protos.shape
    groups, share, _ = pieces[0].shape
    share -= CODE_ROWS
    blocks = lax.axis_size("col")
    crops = blocks * groups * share
    return pl.pallas_call(
        weights_kernel,
        in_specs=[pl.BlockSpec(memory_space=pltpu.SMEM)] + [VMEM_SPEC] * (1 + len(pieces) + len(before)),
        out_specs=[VMEM_SPEC] * 5,
        out_shape=[
            pltpu.VMEM((count, crops), jnp.bfloat16),
            pltpu.VMEM((count, crops), jnp.bfloat16),
            pltpu.VMEM((crops // share, share), jnp.float32),
            pltpu.VMEM((crops, width), jnp.bfloat16),
            pltpu.VMEM((blocks, groups, CODE_ROWS, width), jnp.bfloat16),
        ],
        input_output_aliases={2 + len(pieces) + at: at for at in range(len(before))},
        compiler_params=pltpu.CompilerParams(vmem_limit_bytes=6 << 20),
        cost_estimate=pl.CostEstimate(
            flops=4 * count * groups * share * width,
            bytes_accessed=16 * count * groups * share,
            transcendentals=2 * count * groups * share,
        ),
        name="exp_weights",
    )(places, protos, *pieces, *before)


def balance_kernel(*refs):
    *scale_refs, sink_ref, row_ref, column_ref, sums = refs
    count, crops = sink_ref.shape
    rows, lanes, stride = BALANCE_STEP, 128, 2048
    for at in range(0, count, rows):
        span = pl.ds(at, rows)
        part = jnp.zeros((rows, lanes), jnp.float32)
        for line in range(crops // lanes):
            values = sink_ref[span, pl.ds(line * lanes, lanes)].astype(jnp.float32)
            for scale_ref in scale_refs:
                values = values * scale_ref[pl.ds(line, 1), :]
            part += values
        column = 1.0 / jnp.sum(part, axis=1, keepdims=True)
        column_ref[span, :] = column
        across = jnp.broadcast_to(column, (rows, lanes)).T[:8, :]
        high = across.astype(jnp.bfloat16)
        low = (across - high.astype(jnp.float32)).astype(jnp.bfloat16)
        both = jnp.concatenate([high, low], axis=0)
        for start in range(0, crops, stride):
            columns = pl.ds(start, stride)
            product = jnp.dot(both, sink_ref[span, columns], preferred_element_type=jnp.float32)
            product = product[0:1, :] + product[8:9, :]
            if at == 0:
                sums[:, columns] = product
            else:
                sums[:, columns] += product
    for line in range(crops // lanes):
        row_ref[pl.ds(line, 1), :] = sums[:, pl.ds(line * lanes, lanes)]


def balance(sink_weight, *row_scale):
    count, crops = sink_weight.shape
    return pl.pallas_call(
        balance_kernel,
        in_specs=[VMEM_SPEC] * (1 + len(row_scale)),
        out_specs=[VMEM_SPEC] * 2,
        out_shape=[
            jax.ShapeDtypeStruct((crops // 128, 128), jnp.float32),
            jax.ShapeDtypeStruct((count, 1), jnp.float32),
        ],
        scratch_shapes=[pltpu.VMEM((1, crops), jnp.float32)],
        compiler_params=pltpu.CompilerParams(vmem_limit_bytes=6 << 20),
        cost_estimate=pl.CostEstimate(
            flops=4 * count * crops, bytes_accessed=2 * count * crops, transcendentals=0
        ),
        name="balance",
    )(*row_scale, sink_weight)


def product_kernel(first, finish, scale_ref, rows_ref, weight_ref, *refs):
    *extra, out_ref, scaled = refs
    lanes = 128
    for line in range(rows_ref.shape[0] // lanes):
        span = pl.ds(line * lanes, lanes)
        scale = jnp.broadcast_to(scale_ref[pl.ds(line, 1), :], (lanes, lanes)).T
        for at in range(0, scaled.shape[1], lanes):
            columns = pl.ds(at, lanes)
            values = rows_ref[span, columns].astype(jnp.float32) * scale
            scaled[span, columns] = values.astype(jnp.bfloat16)
    for start in range(0, out_ref.shape[0], PRODUCT_STEP):
        own = pl.ds(first + start, PRODUCT_STEP)
        product = jnp.dot(weight_ref[own, :], scaled[...], preferred_element_type=jnp.float32)
        if finish is not None:
            product = finish(product, *[ref[own, :] for ref in extra])
        out_ref[pl.ds(start, PRODUCT_STEP), :] = product.astype(out_ref.dtype)


def scaled_product(weight, scale, rows, first=0, count=None, finish=None, extra=(), kind=jnp.float32):
    crops = weight.shape[1]
    count = weight.shape[0] if count is None else count
    width = rows.shape[1]
    return pl.pallas_call(
        functools.partial(product_kernel, first, finish),
        in_specs=[VMEM_SPEC] * (3 + len(extra)),
        out_specs=VMEM_SPEC,
        out_shape=jax.ShapeDtypeStruct((count, width), kind),
        scratch_shapes=[pltpu.VMEM((crops, width), jnp.bfloat16)],
        compiler_params=pltpu.CompilerParams(vmem_limit_bytes=8 << 20),
        cost_estimate=pl.CostEstimate(
            flops=2 * count * crops * width,
            bytes_accessed=2 * count * crops + 2 * crops * width,
            transcendentals=0,
        ),
        name="scaled_product",
    )(scale, rows, weight, *extra)


def swap_kernel(code_ref, embed_ref, out_ref):
    cols, blocks, _, width = code_ref.shape
    share = width // 2
    place = lax.broadcasted_iota(jnp.int32, (cols * share, share), 0)
    for block in range(blocks):
        chosen, embed = [], []
        for col in range(cols):
            code = code_ref[col, block].astype(jnp.float32)[0:1, :]
            partner = (CODE_BASE * code[:, :share] + code[:, share:]).astype(jnp.int32)
            chosen.append(jnp.where(place == partner, 1.0, 0.0).astype(jnp.bfloat16))
            embed.append(embed_ref[pl.ds((col * blocks + block) * share, share), :])
        swapped = jnp.dot(
            jnp.concatenate(chosen, axis=1),
            jnp.concatenate(embed, axis=0),
            preferred_element_type=jnp.float32,
        ).astype(jnp.bfloat16)
        for col in range(cols):
            out_ref[pl.ds((col * blocks + block) * share, share), :] = swapped[
                col * share : (col + 1) * share, :
            ]


def swap_partners(codes, embedding):
    crops, width = embedding.shape
    return pl.pallas_call(
        swap_kernel,
        in_specs=[VMEM_SPEC] * 2,
        out_specs=VMEM_SPEC,
        out_shape=pltpu.VMEM((crops, width), jnp.bfloat16),
        compiler_params=pltpu.CompilerParams(vmem_limit_bytes=6 << 20),
        cost_estimate=pl.CostEstimate(
            flops=2 * crops * 1024 * width, bytes_accessed=16 * crops * width, transcendentals=0
        ),
        name="swap_partners",
    )(codes, embedding)


def shards(crop_rows, up_weight, down_weight, proj_weight, prototypes, partner):
    tp_count = lax.axis_size("tp")
    col_count = lax.axis_size("col")
    row_count = lax.axis_size("row")
    crop_values = crop_rows.astype(jnp.float32)
    centred = crop_values - jnp.mean(crop_values, axis=1, keepdims=True)
    normed = (
        centred * lax.rsqrt(jnp.mean(centred * centred, axis=1, keepdims=True) + 1e-05)
    ).astype(jnp.bfloat16)
    hidden = jax.nn.gelu(jnp.dot(normed, up_weight, preferred_element_type=jnp.float32)).astype(
        jnp.bfloat16
    )
    branch_out = jnp.dot(hidden, down_weight, preferred_element_type=jnp.float32)
    partial_proj = jnp.dot(
        crop_values / tp_count + branch_out,
        proj_weight.astype(jnp.float32),
        precision=lax.Precision.HIGHEST,
    )
    embed_width = partial_proj.shape[1]
    block_rows = partner.shape[0]
    proto_total = prototypes.shape[0] * col_count * tp_count
    own_count = prototypes.shape[0] // row_count
    own_rows = lax.dynamic_slice_in_dim(
        prototypes, lax.axis_index("row") * own_count, own_count, 0
    )
    raw_rows = own_rows.astype(jnp.float32)
    unit_protos = unit_rows(raw_rows).astype(jnp.bfloat16)

    local_raw, unit_protos = together(pairwise_sum(partial_proj, "tp"), unit_protos)
    local_embed = unit_rows(local_raw).astype(jnp.bfloat16)
    share = local_embed.shape[0]
    own_partner = lax.dynamic_slice_in_dim(partner, lax.axis_index("col") * share, share)
    own_partner = own_partner - block_rows * lax.axis_index("row")
    code = jnp.stack([own_partner // CODE_BASE, own_partner % CODE_BASE]).astype(jnp.bfloat16)
    code = jnp.pad(code.reshape(1, -1), ((0, CODE_ROWS - 1), (0, 0)))
    local_embed = jnp.concatenate([local_embed, code], axis=0)

    crops = row_count * block_rows
    row, col = lax.axis_index("row"), lax.axis_index("col")
    col_places = [
        (((col + turn) & 7) ^ jnp.arange(2, dtype=jnp.int32)) for turn in (0, 6, 2, 4)
    ]
    row_places = [
        (((row ^ flip) + turn) & 7).astype(jnp.uint32) for flip in (0, 1) for turn in (0, 2, 4, 6)
    ]
    local_embed, *places = together(local_embed, *col_places, *row_places)
    weights = gather_embeddings(
        local_embed,
        places[:4],
        lambda place, pieces, before: list(exp_weights(place, unit_protos, pieces, before)),
    )
    sink_weight, soft_weight, soft_part, embedding, codes = weights
    row_part, column_factor = balance(sink_weight)
    sums = total_sum(jnp.stack([row_part, soft_part]))
    sums, embedding, codes = together(sums, embedding, codes)
    soft_sum = scaled_product(soft_weight, 1.0 / sums[1], embedding)
    soft_sum, embedding, codes = together(soft_sum, embedding, codes)
    swapped = swap_partners(codes, embedding)
    row_scale, soft_sum, swapped = together(1.0 / sums[0], soft_sum, swapped)
    for iteration in range(1, ITERS):
        row_part, column_factor = balance(sink_weight, row_scale)
        row_scale = 1.0 / total_sum(row_part[None])[0]

    out_scale = embed_width / math.sqrt(crops)

    def gradient(target_part, soft_part, column, protos):
        raw = protos.astype(jnp.float32)
        summed = proto_total * (soft_part - column * target_part)
        square_mean = jnp.mean(raw * raw, axis=1, keepdims=True)
        factor = lax.rsqrt(embed_width * (square_mean + 1e-06))
        inner_prod = jnp.sum(raw * summed, axis=1, keepdims=True)
        result = factor * summed - factor * raw * inner_prod / (
            embed_width * (square_mean + 1e-06)
        )
        return out_scale * result

    def own_half(first, scale):
        return scaled_product(
            sink_weight,
            scale,
            swapped,
            first,
            own_count // 2,
            gradient,
            (soft_sum, column_factor, own_rows),
            jnp.bfloat16,
        )

    return gather_rows(own_half(0, row_scale), own_half(own_count // 2, row_scale), places[4:])


def solution(mesh):
    return jax.shard_map(
        shards,
        mesh=mesh,
        in_specs=(
            P(("row", "col"), None),
            P(None, "tp"),
            P("tp", None),
            P(),
            P(("col", "tp"), None),
            P("row"),
        ),
        out_specs=P(("col", "tp"), None),
        check_vma=False,
    )
```

```python
import functools
import math

import jax
import jax.numpy as jnp
from jax import lax
from jax.experimental import pallas as pl
from jax.experimental.pallas import tpu as pltpu
from jax.sharding import PartitionSpec as P

ITERS = 3


SOFTMAX_TEMPER = 0.1
LOG2_E = 1.4426950408889634
CROP_STEP = 512
PROTO_STEP = 256
BALANCE_STEP = 128
PRODUCT_STEP = 256
CODE_ROWS = 16
CODE_BASE = 32


def unit_rows(matrix):
    square_mean = jnp.mean(matrix * matrix, axis=-1, keepdims=True)
    return matrix * lax.rsqrt(matrix.shape[-1] * (square_mean + 1e-06))


def shifted(block, axis, target):
    count = lax.axis_size(axis)
    return lax.ppermute(block, axis, [(device, target(device) % count) for device in range(count)])


def placed(pieces, count):
    rows = pieces[0][0].shape
    result = jnp.zeros((count,) + rows, pieces[0][0].dtype)
    for piece, place in pieces:
        result = lax.dynamic_update_slice_in_dim(result, piece[None], place, 0)
    return result


def pairwise_sum(block, axis):
    count = lax.axis_size(axis)
    terms = [block] + [
        shifted(block, axis, lambda device, step=step: device ^ step) for step in range(1, count)
    ]
    while len(terms) > 1:
        terms = [terms[at] + terms[at + 1] for at in range(0, len(terms), 2)]
    return terms[0]


def together(*values):
    return lax.optimization_barrier(values)


def spread_kernel(terms_ref, out_ref):
    total = jnp.sum(terms_ref[...].astype(jnp.float32), axis=0).astype(out_ref.dtype)
    for at in range(out_ref.shape[0]):
        out_ref[at] = total


def sum_and_copies(terms, count, kind):
    vmem = pl.BlockSpec(memory_space=pltpu.VMEM)
    return pl.pallas_call(
        spread_kernel,
        in_specs=[vmem],
        out_specs=vmem,
        out_shape=jax.ShapeDtypeStruct((count,) + terms.shape[1:], kind),
        compiler_params=pltpu.CompilerParams(vmem_limit_bytes=4 << 20),
        name="sum_and_copies",
    )(terms)


def exchanged(blocks, axes):
    return lax.all_to_all(blocks, axes, 0, 0, tiled=True)


def total_sum(parts):
    count, lines, lanes = parts.shape
    cols, others = lax.axis_size("col"), lax.axis_size(("row", "tp"))
    share = lines // cols
    scattered = jnp.swapaxes(parts.reshape(count, cols, share, lanes), 0, 1)
    scattered = scattered.reshape(cols, count * share, lanes)
    kind = jnp.float32 if count == 1 else jnp.bfloat16
    own = sum_and_copies(exchanged(scattered, "col"), others, kind)
    own = sum_and_copies(exchanged(own, ("row", "tp")), cols, jnp.float32)
    gathered = exchanged(own, "col").reshape(cols, count, share, lanes)
    return jnp.swapaxes(gathered, 0, 1).reshape(count, lines, lanes)


def gather_embeddings(local_embed, places, weigh):
    row = lax.axis_index("row")
    far = shifted(local_embed, "row", lambda device: device ^ 1)
    pair = placed([(local_embed, row & 1), (far, 1 - (row & 1))], 2)
    line = [
        (pair, row >> 1),
        (shifted(pair, "row", lambda device: device + 2), ((row >> 1) + 3) & 3),
        (shifted(pair, "row", lambda device: device - 2), ((row >> 1) + 1) & 3),
        (shifted(pair, "row", lambda device: device + 4), ((row >> 1) + 2) & 3),
    ]
    block = placed(line, 4).reshape((-1,) + local_embed.shape)
    swap = lambda piece: shifted(piece, "col", lambda device: device ^ 1)
    others = [
        shifted(block, "col", lambda device: device + 2),
        shifted(block, "col", lambda device: device - 2),
        shifted(block, "col", lambda device: device + 4),
    ]
    twin = swap(block)
    weights = weigh(places[0], (block, twin), [])
    *pieces, weights[2] = together(*others, weights[2])
    twins = [swap(piece) for piece in pieces]
    for place, piece, twin in zip(places[1:], pieces, twins):
        weights = weigh(place, (piece, twin), weights)
    return weights


def put_kernel(turns, starts, place_ref, *refs):
    pieces = refs[: len(starts)]
    out_ref, landed = refs[-2:]
    copies = []
    for at, (piece, start) in enumerate(zip(pieces, starts)):
        span = pl.ds(start, piece.shape[0])
        copies.append(
            pltpu.make_async_copy(piece, out_ref.at[place_ref[turns[at]], span], landed.at[at])
        )
        copies[at].start()
    for copy in copies:
        copy.wait()


def put_pieces(places, before, shape, pieces):
    blocks, turns, starts = zip(*pieces)
    anywhere = pl.BlockSpec(memory_space=pl.ANY)
    return pl.pallas_call(
        functools.partial(put_kernel, turns, starts),
        in_specs=[pl.BlockSpec(memory_space=pltpu.SMEM)]
        + [anywhere] * (len(blocks) + len(before)),
        out_specs=anywhere,
        out_shape=jax.ShapeDtypeStruct(shape, blocks[0].dtype),
        scratch_shapes=[pltpu.SemaphoreType.DMA((len(blocks),))],
        input_output_aliases={1 + len(blocks): 0} if before else {},
        compiler_params=pltpu.CompilerParams(vmem_limit_bytes=4 << 20),
        cost_estimate=pl.CostEstimate(
            flops=0, bytes_accessed=2 * sum(block.size * 2 for block in blocks), transcendentals=0
        ),
        name="put_pieces",
    )(places, *blocks, *before)


def gather_rows(own0, own1, places):
    half, width = own0.shape
    quarter = half // 2
    shape = (8, 2 * half, width)
    near, over = range(4), range(4, 8)
    flip = lambda block: shifted(block, "row", lambda device: device ^ 1)
    right = lambda block: shifted(block, "row", lambda device: device + 2)
    left = lambda block: shifted(block, "row", lambda device: device - 2)

    far0, near0_r, near0_l = flip(own0), right(own0), left(own0)
    far1, near1_r, near1_l = flip(own1), right(own1), left(own1)
    far0, near0_r, near0_l, near1_r, near1_l = together(far0, near0_r, near0_l, near1_r, near1_l)
    far0_r, far0_l, opp0, opp1 = right(far0), left(far0), right(near0_r), left(near1_l)
    pieces = [
        (own0, near[0], 0),
        (own1, near[0], half),
        (near0_r, near[3], 0),
        (near0_l, near[1], 0),
        (far0, over[0], 0),
        (near1_r, near[3], half),
        (near1_l, near[1], half),
    ]
    result = put_pieces(places, [], shape, pieces)
    result, far1, far0_r, far0_l, opp0, opp1 = together(result, far1, far0_r, far0_l, opp0, opp1)
    far1_r, far1_l = right(far1), left(far1)
    far0_or, far0_ol = right(far0_r[:quarter]), left(far0_l[quarter:])
    pieces = [
        (opp0, near[2], 0),
        (opp1, near[2], half),
        (far0_r, over[3], 0),
        (far0_l, over[1], 0),
        (far1, over[0], half),
    ]
    result = put_pieces(places, [result], shape, pieces)
    result, far1_r, far1_l, far0_or, far0_ol = together(result, far1_r, far1_l, far0_or, far0_ol)
    far1_or, far1_ol = right(far1_r[:quarter]), left(far1_l[quarter:])
    pieces = [
        (far0_or, over[2], 0),
        (far0_ol, over[2], quarter),
        (far1_r, over[3], half),
        (far1_l, over[1], half),
    ]
    result = put_pieces(places, [result], shape, pieces)
    result, far1_or, far1_ol = together(result, far1_or, far1_ol)
    result = put_pieces(
        places, [result], shape, [(far1_or, over[2], half), (far1_ol, over[2], half + quarter)]
    )
    return result.reshape(-1, width)


def weights_kernel(place_ref, protos_ref, *refs):
    sink_ref, soft_ref, total_ref, copy_ref, code_ref = refs[-5:]
    for at in range(place_ref.shape[0]):
        embed_ref = refs[at]
        groups, share, width = embed_ref.shape
        share -= CODE_ROWS
        place = place_ref[at]
        per_step = CROP_STEP // share
        code_ref[pl.ds(place, 1)] = embed_ref[:, share:, :][None]
        for group in range(0, groups, per_step):
            columns = pl.ds(pl.multiple_of((place * groups + group) * share, CROP_STEP), CROP_STEP)
            embed = embed_ref[group : group + per_step, :share, :].reshape(CROP_STEP, width)
            copy_ref[columns, :] = embed
            total = jnp.zeros((1, CROP_STEP), jnp.float32)
            for start in range(0, protos_ref.shape[0], PROTO_STEP):
                rows = pl.ds(start, PROTO_STEP)
                score = lax.dot_general(
                    protos_ref[rows, :],
                    embed,
                    (((1,), (1,)), ((), ())),
                    preferred_element_type=jnp.float32,
                )
                weight = jnp.exp2(score * (LOG2_E / SOFTMAX_TEMPER))
                soft_ref[rows, columns] = weight.astype(jnp.bfloat16)
                sink_ref[rows, columns] = (weight * weight).astype(jnp.bfloat16)
                total += jnp.sum(weight, axis=0, keepdims=True)
            for line in range(per_step):
                total_ref[pl.ds(place * groups + group + line, 1), :] = total[
                    :, line * share : (line + 1) * share
                ]


VMEM_SPEC = pl.BlockSpec(memory_space=pltpu.VMEM)


def exp_weights(places, protos, pieces, before):
    count, width = protos.shape
    groups, share, _ = pieces[0].shape
    share -= CODE_ROWS
    blocks = lax.axis_size("col")
    crops = blocks * groups * share
    return pl.pallas_call(
        weights_kernel,
        in_specs=[pl.BlockSpec(memory_space=pltpu.SMEM)] + [VMEM_SPEC] * (1 + len(pieces) + len(before)),
        out_specs=[VMEM_SPEC] * 5,
        out_shape=[
            pltpu.VMEM((count, crops), jnp.bfloat16),
            pltpu.VMEM((count, crops), jnp.bfloat16),
            pltpu.VMEM((crops // share, share), jnp.float32),
            pltpu.VMEM((crops, width), jnp.bfloat16),
            pltpu.VMEM((blocks, groups, CODE_ROWS, width), jnp.bfloat16),
        ],
        input_output_aliases={2 + len(pieces) + at: at for at in range(len(before))},
        compiler_params=pltpu.CompilerParams(vmem_limit_bytes=6 << 20),
        cost_estimate=pl.CostEstimate(
            flops=4 * count * groups * share * width,
            bytes_accessed=16 * count * groups * share,
            transcendentals=2 * count * groups * share,
        ),
        name="exp_weights",
    )(places, protos, *pieces, *before)


def balance_kernel(kept, *refs):
    *scale_refs, sink_ref, row_ref, column_ref, sums = refs[kept:]
    count, crops = sink_ref.shape
    rows, lanes, stride = BALANCE_STEP, 128, 2048
    for at in range(0, count, rows):
        span = pl.ds(at, rows)
        part = jnp.zeros((rows, lanes), jnp.float32)
        for line in range(crops // lanes):
            values = sink_ref[span, pl.ds(line * lanes, lanes)].astype(jnp.float32)
            for scale_ref in scale_refs:
                values = values * scale_ref[pl.ds(line, 1), :]
            part += values
        column = 1.0 / jnp.sum(part, axis=1, keepdims=True)
        column_ref[span, :] = column
        across = jnp.broadcast_to(column, (rows, lanes)).T[:8, :]
        high = across.astype(jnp.bfloat16)
        low = (across - high.astype(jnp.float32)).astype(jnp.bfloat16)
        both = jnp.concatenate([high, low], axis=0)
        for start in range(0, crops, stride):
            columns = pl.ds(start, stride)
            product = jnp.dot(both, sink_ref[span, columns], preferred_element_type=jnp.float32)
            product = product[0:1, :] + product[8:9, :]
            if at == 0:
                sums[:, columns] = product
            else:
                sums[:, columns] += product
    for line in range(crops // lanes):
        row_ref[pl.ds(line, 1), :] = sums[:, pl.ds(line * lanes, lanes)]


def balance(sink_weight, *row_scale, kept=()):
    count, crops = sink_weight.shape
    return pl.pallas_call(
        functools.partial(balance_kernel, len(kept)),
        in_specs=[VMEM_SPEC] * (1 + len(row_scale) + len(kept)),
        out_specs=[VMEM_SPEC] * 2,
        out_shape=[
            jax.ShapeDtypeStruct((crops // 128, 128), jnp.float32),
            jax.ShapeDtypeStruct((count, 1), jnp.float32),
        ],
        scratch_shapes=[pltpu.VMEM((1, crops), jnp.float32)],
        compiler_params=pltpu.CompilerParams(vmem_limit_bytes=6 << 20),
        cost_estimate=pl.CostEstimate(
            flops=4 * count * crops, bytes_accessed=2 * count * crops, transcendentals=0
        ),
        name="balance",
    )(*kept, *row_scale, sink_weight)


def product_kernel(first, finish, scale_ref, rows_ref, weight_ref, *refs):
    *extra, out_ref, scaled = refs
    lanes = 128
    for line in range(rows_ref.shape[0] // lanes):
        span = pl.ds(line * lanes, lanes)
        scale = jnp.broadcast_to(scale_ref[pl.ds(line, 1), :], (lanes, lanes)).T
        for at in range(0, scaled.shape[1], lanes):
            columns = pl.ds(at, lanes)
            values = rows_ref[span, columns].astype(jnp.float32) * scale
            scaled[span, columns] = values.astype(jnp.bfloat16)
    for start in range(0, out_ref.shape[0], PRODUCT_STEP):
        own = pl.ds(first + start, PRODUCT_STEP)
        product = jnp.dot(weight_ref[own, :], scaled[...], preferred_element_type=jnp.float32)
        if finish is not None:
            product = finish(product, *[ref[own, :] for ref in extra])
        out_ref[pl.ds(start, PRODUCT_STEP), :] = product.astype(out_ref.dtype)


def scaled_product(weight, scale, rows, first=0, count=None, finish=None, extra=(), kind=jnp.float32):
    crops = weight.shape[1]
    count = weight.shape[0] if count is None else count
    width = rows.shape[1]
    return pl.pallas_call(
        functools.partial(product_kernel, first, finish),
        in_specs=[VMEM_SPEC] * (3 + len(extra)),
        out_specs=VMEM_SPEC,
        out_shape=jax.ShapeDtypeStruct((count, width), kind),
        scratch_shapes=[pltpu.VMEM((crops, width), jnp.bfloat16)],
        compiler_params=pltpu.CompilerParams(vmem_limit_bytes=8 << 20),
        cost_estimate=pl.CostEstimate(
            flops=2 * count * crops * width,
            bytes_accessed=2 * count * crops + 2 * crops * width,
            transcendentals=0,
        ),
        name="scaled_product",
    )(scale, rows, weight, *extra)


def swap_kernel(code_ref, embed_ref, out_ref):
    cols, blocks, _, width = code_ref.shape
    share = width // 2
    place = lax.broadcasted_iota(jnp.int32, (cols * share, share), 0)
    for block in range(blocks):
        chosen, embed = [], []
        for col in range(cols):
            code = code_ref[col, block].astype(jnp.float32)[0:1, :]
            partner = (CODE_BASE * code[:, :share] + code[:, share:]).astype(jnp.int32)
            chosen.append(jnp.where(place == partner, 1.0, 0.0).astype(jnp.bfloat16))
            embed.append(embed_ref[pl.ds((col * blocks + block) * share, share), :])
        swapped = jnp.dot(
            jnp.concatenate(chosen, axis=1),
            jnp.concatenate(embed, axis=0),
            preferred_element_type=jnp.float32,
        ).astype(jnp.bfloat16)
        for col in range(cols):
            out_ref[pl.ds((col * blocks + block) * share, share), :] = swapped[
                col * share : (col + 1) * share, :
            ]


def swap_partners(codes, embedding):
    crops, width = embedding.shape
    return pl.pallas_call(
        swap_kernel,
        in_specs=[VMEM_SPEC] * 2,
        out_specs=VMEM_SPEC,
        out_shape=pltpu.VMEM((crops, width), jnp.bfloat16),
        compiler_params=pltpu.CompilerParams(vmem_limit_bytes=6 << 20),
        cost_estimate=pl.CostEstimate(
            flops=2 * crops * 1024 * width, bytes_accessed=16 * crops * width, transcendentals=0
        ),
        name="swap_partners",
    )(codes, embedding)


def shards(crop_rows, up_weight, down_weight, proj_weight, prototypes, partner):
    tp_count = lax.axis_size("tp")
    col_count = lax.axis_size("col")
    row_count = lax.axis_size("row")
    crop_values = crop_rows.astype(jnp.float32)
    centred = crop_values - jnp.mean(crop_values, axis=1, keepdims=True)
    normed = (
        centred * lax.rsqrt(jnp.mean(centred * centred, axis=1, keepdims=True) + 1e-05)
    ).astype(jnp.bfloat16)
    hidden = jax.nn.gelu(jnp.dot(normed, up_weight, preferred_element_type=jnp.float32)).astype(
        jnp.bfloat16
    )
    branch_out = jnp.dot(hidden, down_weight, preferred_element_type=jnp.float32)
    partial_proj = jnp.dot(
        crop_values / tp_count + branch_out,
        proj_weight.astype(jnp.float32),
        precision=lax.Precision.HIGHEST,
    )
    embed_width = partial_proj.shape[1]
    block_rows = partner.shape[0]
    proto_total = prototypes.shape[0] * col_count * tp_count
    own_count = prototypes.shape[0] // row_count
    own_rows = lax.dynamic_slice_in_dim(
        prototypes, lax.axis_index("row") * own_count, own_count, 0
    )
    raw_rows = own_rows.astype(jnp.float32)
    unit_protos = unit_rows(raw_rows).astype(jnp.bfloat16)

    local_raw, unit_protos = together(pairwise_sum(partial_proj, "tp"), unit_protos)
    local_embed = unit_rows(local_raw).astype(jnp.bfloat16)
    share = local_embed.shape[0]
    own_partner = lax.dynamic_slice_in_dim(partner, lax.axis_index("col") * share, share)
    own_partner = own_partner - block_rows * lax.axis_index("row")
    code = jnp.stack([own_partner // CODE_BASE, own_partner % CODE_BASE]).astype(jnp.bfloat16)
    code = jnp.pad(code.reshape(1, -1), ((0, CODE_ROWS - 1), (0, 0)))
    local_embed = jnp.concatenate([local_embed, code], axis=0)

    crops = row_count * block_rows
    row, col = lax.axis_index("row"), lax.axis_index("col")
    col_places = [
        (((col + turn) & 7) ^ jnp.arange(2, dtype=jnp.int32)) for turn in (0, 6, 2, 4)
    ]
    order = jnp.arange(8, dtype=jnp.int32)
    row_places = ((row ^ (order >> 2)) + 2 * (order & 3)) & 7
    local_embed, *places = together(local_embed, *col_places, row_places)
    weights = gather_embeddings(
        local_embed,
        places[:4],
        lambda place, pieces, before: list(exp_weights(place, unit_protos, pieces, before)),
    )
    sink_weight, soft_weight, soft_part, embedding, codes = weights
    row_part, column_factor = balance(sink_weight, kept=(soft_weight,))
    sums = total_sum(jnp.stack([row_part, soft_part]))
    sums, embedding, codes = together(sums, embedding, codes)
    soft_sum = scaled_product(soft_weight, 1.0 / sums[1], embedding)
    soft_sum, embedding, codes = together(soft_sum, embedding, codes)
    swapped = swap_partners(codes, embedding)
    row_scale, soft_sum, swapped = together(1.0 / sums[0], soft_sum, swapped)
    for iteration in range(1, ITERS):
        row_part, column_factor = balance(sink_weight, row_scale)
        row_scale = 1.0 / total_sum(row_part[None])[0]

    out_scale = embed_width / math.sqrt(crops)

    def gradient(target_part, soft_part, column, protos):
        raw = protos.astype(jnp.float32)
        summed = proto_total * (soft_part - column * target_part)
        square_mean = jnp.mean(raw * raw, axis=1, keepdims=True)
        factor = lax.rsqrt(embed_width * (square_mean + 1e-06))
        inner_prod = jnp.sum(raw * summed, axis=1, keepdims=True)
        result = factor * summed - factor * raw * inner_prod / (
            embed_width * (square_mean + 1e-06)
        )
        return out_scale * result

    def own_half(first, scale):
        return scaled_product(
            sink_weight,
            scale,
            swapped,
            first,
            own_count // 2,
            gradient,
            (soft_sum, column_factor, own_rows),
            jnp.bfloat16,
        )

    return gather_rows(own_half(0, row_scale), own_half(own_count // 2, row_scale), places[4])


def solution(mesh):
    return jax.shard_map(
        shards,
        mesh=mesh,
        in_specs=(
            P(("row", "col"), None),
            P(None, "tp"),
            P("tp", None),
            P(),
            P(("col", "tp"), None),
            P("row"),
        ),
        out_specs=P(("col", "tp"), None),
        check_vma=False,
    )
```
